128 devices in a mesh: doc: 32 (over x, z, core), bkt: 4 (over y).
Axes of the slice: x: 4, y: 4, z: 4, core: 2. Of those that a mesh axis runs over, the one named last changes fastest.
Arguments:
- start_vectors: float32 [64, 131072], P(None, ('doc', 'bkt')), may hold values from -6 to 6
- bucket_weight: float32 [32768], P('bkt'), may hold values from 0.1 to 1
- tile_count: int32 [32, 4], P('doc', 'bkt'), may hold values from 128 to 256, as said below
- tile_coords: int32 [32, 4, 256, 2], P('doc', 'bkt'), may hold values from 0 to 63, as said below
- patterns: int32 [32, 4, 256, 128, 128], P('doc', 'bkt'), may hold values from 0 to 1
Outputs:
- eigen_block: float32 [64, 131072], P(None, ('doc', 'bkt'))
The draws below stay inside these ranges and needn't reach their ends.
Inputs may be any that keep to these rules, and one draw needn't show every extreme that they name: `tile_count`: the largest count is exactly 256 in every draw. `tile_coords`: row tiles lie below 32, column tiles below 64; the pairs of one document band and bucket band are distinct.
All inputs are finite; a program needn't handle non-finite values.
Results may differ from the reference program's by a relative error of at most 0.018.
Values may be sent and summed in bfloat16 or wider, within the bound.
No kernel may reach another device: no remote copies, remote signals or barrier semaphores. Data moves between devices by JAX's collectives and lax.ppermute only.
A program may use at most 128 MiB of HBM per device.

```python
import math
import jax
import jax.numpy as jnp
from jax import lax

K = 64
TILE = 128
ITERS = 2
DOC_BAND = 4096
TMAX = 256
DOC_BANDS = 32
BKT_BANDS = 4
BKT_BAND = 8192
NDOC = 131072
NBKT = 32768


def draw_tile_count(key, part):
    device_total = DOC_BANDS * BKT_BANDS
    base = jax.random.randint(jax.random.fold_in(key, 21), (device_total,), TMAX // 2, TMAX + 1)
    fullest = jax.random.randint(jax.random.fold_in(key, 22), (), 0, device_total)
    counts = jnp.where(jnp.arange(device_total) == fullest, TMAX, base)
    return counts.reshape(DOC_BANDS, BKT_BANDS).astype(jnp.int32)


def draw_tile_coords(key, part):
    row_tiles = DOC_BAND // TILE
    col_tiles = BKT_BAND // TILE
    keys = jax.random.split(jax.random.fold_in(key, 11), DOC_BANDS * BKT_BANDS)
    picks = jax.vmap(lambda single: jax.random.permutation(single, row_tiles * col_tiles)[:TMAX])(keys)
    coords = jnp.stack([picks // col_tiles, picks % col_tiles], axis=-1)
    return coords.reshape(DOC_BANDS, BKT_BANDS, TMAX, 2).astype(jnp.int32)


def draw_patterns(key, part):
    shape_rows = (DOC_BANDS, BKT_BANDS, TMAX, TILE, 1)
    shape_full = (DOC_BANDS, BKT_BANDS, TMAX, TILE, TILE)
    levels = jax.random.randint(jax.random.fold_in(key, 31), shape_rows, 1, 17)
    values = jax.random.randint(jax.random.fold_in(key, 32), shape_full, 0, 256)
    return (values < levels).astype(jnp.int32)


def shard_levels(key, dims, shards, low, largest):
    level = 1.0
    for axis_at, blocks in shards:
        draws = jax.random.uniform(jax.random.fold_in(jax.random.fold_in(key, 6), axis_at), (blocks,), jnp.float32, low / len(shards), largest / len(shards))
        level = level * jnp.repeat(jnp.exp(draws), dims[axis_at] // blocks).reshape((-1,) + (1,) * (len(dims) - 1 - axis_at))
    return level


def gaussian(key, extent, width, reach, cuts=(), kind=jnp.bfloat16):
    drawn = width * jax.random.normal(key, extent, jnp.float32)
    if cuts:
        drawn = drawn * shard_levels(key, extent, cuts, -0.22, 0.18)
    return jnp.clip(drawn, -reach, reach).astype(kind)


def setup_inputs(seed: int = 0) -> dict:
    key_list = jax.random.split(jax.random.key(seed), 6)
    start_vectors = gaussian(key_list[0], (K, NDOC), 1.0, 6.0, ((1, 128),), jnp.float32)
    bucket_weight = jnp.clip(jnp.exp(math.log(1.0) - 2.3025851 * jax.random.uniform(key_list[1], (NBKT,), jnp.float32) ** shard_levels(key_list[1], (NBKT,), ((0, 4),), -0.2, 0.2)), 0.1, 1.0)
    tile_count = draw_tile_count(jax.random.fold_in(key_list[5], 71), 0)
    tile_coords = draw_tile_coords(jax.random.fold_in(key_list[5], 71), 0)
    patterns = draw_patterns(jax.random.fold_in(key_list[5], 71), 0)
    return dict(start_vectors=start_vectors, bucket_weight=bucket_weight, tile_count=tile_count, tile_coords=tile_coords, patterns=patterns)


def reference(start_vectors, bucket_weight, tile_count, tile_coords, patterns):
    row_tiles = DOC_BAND // TILE
    col_tiles = BKT_BAND // TILE
    device_total = DOC_BANDS * BKT_BANDS
    band_doc = jnp.repeat(jnp.arange(DOC_BANDS, dtype=jnp.int32), BKT_BANDS)
    band_bkt = jnp.tile(jnp.arange(BKT_BANDS, dtype=jnp.int32), DOC_BANDS)
    coords = tile_coords.reshape(device_total, TMAX, 2)
    global_rows = (band_doc[:, None] * row_tiles + coords[:, :, 0]).astype(jnp.int32)
    global_cols = (band_bkt[:, None] * col_tiles + coords[:, :, 1]).astype(jnp.int32)
    live_slot = jnp.arange(TMAX, dtype=jnp.int32)[None, :] < tile_count.reshape(device_total)[:, None]
    tiles_all = patterns.reshape(device_total, TMAX, TILE, TILE)
    items = (tiles_all, global_rows, global_cols, live_slot)
    weight_tiles = bucket_weight.reshape(NBKT // TILE, TILE)

    def masked_tiles(tiles, live):
        return jnp.where(live[:, None, None], tiles, 0).astype(jnp.float32)

    def degree_step(carry, item):
        doc_sum, bucket_sum = carry
        tiles, rows, cols, live = item
        masked = masked_tiles(tiles, live)
        row_part = jnp.einsum('tij,tj->ti', masked, weight_tiles[cols], precision=lax.Precision.HIGHEST)
        doc_sum = doc_sum.at[rows].add(row_part)
        bucket_sum = bucket_sum.at[cols].add(lax.optimization_barrier(jnp.sum(masked, axis=1)))
        return ((doc_sum, bucket_sum), None)
    start = (jnp.zeros((NDOC // TILE, TILE), jnp.float32), jnp.zeros((NBKT // TILE, TILE), jnp.float32))
    (doc_sum, bucket_sum), _ = lax.scan(degree_step, start, items)
    inv_doc = 1.0 / jnp.sqrt(jnp.maximum(doc_sum.reshape(NDOC), 1.0))
    bucket_scale = bucket_weight / jnp.maximum(bucket_sum.reshape(NBKT), 1.0)
    block = start_vectors
    for sweep_index in range(ITERS):
        scaled = (block * inv_doc[None, :]).astype(jnp.bfloat16)
        scaled_tiles = scaled.reshape(K, NDOC // TILE, TILE)

        def forward_step(carry, item):
            tiles, rows, cols, live = item
            masked = masked_tiles(tiles, live)
            picked = scaled_tiles[:, rows, :].astype(jnp.float32)
            terms = jnp.einsum('kti,tij->ktj', picked, masked, precision=lax.Precision.HIGHEST)
            return (carry.at[:, cols, :].add(terms), None)
        panel, _ = lax.scan(forward_step, jnp.zeros((K, NBKT // TILE, TILE), jnp.float32), items)
        weighted = (panel.reshape(K, NBKT) * bucket_scale[None, :]).astype(jnp.bfloat16)
        weighted_tiles = weighted.reshape(K, NBKT // TILE, TILE)

        def backward_step(carry, item):
            tiles, rows, cols, live = item
            masked = masked_tiles(tiles, live)
            picked = weighted_tiles[:, cols, :].astype(jnp.float32)
            terms = jnp.einsum('ktj,tij->kti', picked, masked, precision=lax.Precision.HIGHEST)
            return (carry.at[:, rows, :].add(terms), None)
        image, _ = lax.scan(backward_step, jnp.zeros((K, NDOC // TILE, TILE), jnp.float32), items)
        image = image.reshape(K, NDOC) * inv_doc[None, :]
        gram_matrix = jnp.dot(image, image.T, precision=lax.Precision.HIGHEST) / NDOC
        factor = jnp.linalg.cholesky(gram_matrix)
        block = lax.linalg.triangular_solve(factor, image, left_side=True, lower=True)
    return block
```

```python
import functools

import jax
import jax.numpy as jnp
from jax import lax
from jax.experimental import pallas as pl
from jax.experimental.pallas import tpu as pltpu
from jax.sharding import Mesh
from jax.sharding import PartitionSpec as P

ITERS = 2
K = 64
TILE = 128
SLOTS = 256
ROW_TILES = 32
COL_TILES = 64
TOTAL_DOCS = 131072
OWN = 8
CHUNK = OWN * K
COUNT_ROWS = 16
UNROLL = 32
PREP_STEP = 32
MIB = 1 << 20

X, Z, CORE, BKT = "doc_0", "doc_1", "doc_2", "bkt"
DOC = (X, Z, CORE)
DOC_BKT = (X, Z, CORE, BKT)

f32 = jnp.float32
bf16 = jnp.bfloat16
SMEM = pl.BlockSpec(memory_space=pltpu.SMEM)
VMEM = pl.BlockSpec(memory_space=pltpu.VMEM)
HIGHEST = lax.Precision.HIGHEST


def shape(*lengths, dtype=f32):
    return jax.ShapeDtypeStruct(lengths, dtype)


def call(kernel, name, out_shape, in_specs, scratch=(), limit=8, flops=0, moved=0):
    return pl.pallas_call(
        kernel,
        out_shape=out_shape,
        in_specs=in_specs,
        out_specs=jax.tree.map(lambda _: VMEM, out_shape),
        scratch_shapes=list(scratch),
        compiler_params=pltpu.CompilerParams(vmem_limit_bytes=limit * MIB),
        cost_estimate=pl.CostEstimate(flops=flops, bytes_accessed=moved, transcendentals=0),
        name=name,
    )


def swap(value, axis, mask):
    size = lax.axis_size(axis)
    return lax.ppermute(value, axis, [(i, i ^ mask) for i in range(size)])


def place_of(place):
    return place[0], place[1], place[2], place[3], place[4]


def tile_rows(k):
    return slice(k * K, (k + 1) * K)


def cast_kernel(vectors, out):
    for k in range(OWN):
        out[tile_rows(k), :] = vectors[:, k * TILE : (k + 1) * TILE].astype(bf16)


def prep_kernel(place, coords, weight, pattern_in, pattern, doc_part, size_part, split, doc_acc, size_acc):
    step = pl.program_id(0)

    @pl.when(step == 0)
    def _():
        whole = weight[...]
        high = whole.astype(bf16).astype(f32)
        rest = whole - high
        middle = rest.astype(bf16).astype(f32)
        low = rest - middle
        rows = lax.broadcasted_iota(jnp.int32, split.shape, 1)
        spread = lambda part: jnp.broadcast_to(part[:, None, :], split.shape)
        terms = jnp.where(rows == 2, spread(low), 0.0)
        terms = jnp.where(rows == 1, spread(middle), terms)
        split[...] = jnp.where(rows == 0, spread(high), terms).astype(bf16)
        doc_acc[...] = jnp.zeros_like(doc_acc)
        size_acc[...] = jnp.zeros_like(size_acc)

    count = place[4]
    group = PREP_STEP
    for first in range(0, PREP_STEP, group):
        products, sums = [], []
        for u in range(first, first + group):
            slot = step * PREP_STEP + u
            tile = jnp.where(slot < count, pattern_in[u], 0).astype(f32)
            sums.append(jnp.sum(tile.reshape(TILE // 8, 8, TILE), axis=0))
            tile = tile.astype(bf16)
            pattern[u] = tile
            products.append(
                lax.dot_general(
                    split[coords[2 * slot + 1]],
                    tile,
                    (((1,), (1,)), ((), ())),
                    preferred_element_type=f32,
                )
            )
        for u in range(first, first + group):
            slot = step * PREP_STEP + u
            doc_acc[coords[2 * slot]] += products[u - first]
            size_acc[coords[2 * slot + 1]] += sums[u - first]

    @pl.when(step == pl.num_programs(0) - 1)
    def _():
        doc_part[...] = jnp.sum(doc_acc[...], axis=1)
        size_part[...] = jnp.sum(size_acc[...], axis=1)


def prep(place, coords, weight, patterns):
    block = pl.BlockSpec((PREP_STEP, TILE, TILE), lambda i: (i, 0, 0))
    return pl.pallas_call(
        prep_kernel,
        grid=(SLOTS // PREP_STEP,),
        out_shape=(
            shape(SLOTS, TILE, TILE, dtype=bf16),
            shape(ROW_TILES, TILE),
            shape(COL_TILES, TILE),
        ),
        in_specs=[SMEM, SMEM, VMEM, block],
        out_specs=(block, VMEM, VMEM),
        scratch_shapes=[
            pltpu.VMEM((COL_TILES, 16, TILE), bf16),
            pltpu.VMEM((ROW_TILES, 16, TILE), f32),
            pltpu.VMEM((COL_TILES, 8, TILE), f32),
        ],
        compiler_params=pltpu.CompilerParams(vmem_limit_bytes=16 * MIB),
        cost_estimate=pl.CostEstimate(flops=10**9, bytes_accessed=24 * MIB, transcendentals=0),
        name="prep",
    )(place, coords, weight, patterns)


def tile_products(coords, pattern, source, acc, forward):
    acc[...] = jnp.zeros_like(acc)
    contract = (((1,), (0,)), ((), ())) if forward else (((1,), (1,)), ((), ()))

    def group(g, carry):
        products = []
        for u in range(UNROLL):
            slot = g * UNROLL + u
            at = coords[2 * slot + (0 if forward else 1)]
            products.append(
                lax.dot_general(source[at], pattern[slot], contract, preferred_element_type=f32)
            )
        for u in range(UNROLL):
            slot = g * UNROLL + u
            acc[coords[2 * slot + (1 if forward else 0)]] += products[u]
        return carry

    lax.fori_loop(0, SLOTS // UNROLL, group, 0)


def forward_kernel(first, *refs):
    if first:
        place, coords, x0, x1, x2, x3, d0, d1, d2, d3, sizes, pattern, keep, send, inv, source, acc = refs
    else:
        place, coords, x0, x1, x2, x3, pattern, keep, send, source, acc = refs
    x, z, c, y, _ = place_of(place)
    if first:
        inv[...] = 1.0 / jnp.sqrt(jnp.maximum((d0[...] + d1[...]) + (d2[...] + d3[...]), 1.0))
    for s, block in enumerate((x0, x1, x2, x3)):
        base = (y ^ s) * OWN
        for k in range(OWN):
            tile = block[tile_rows(k), :]
            if first:
                tile = (tile.astype(f32) * inv[pl.ds(base + k, 1), :]).astype(bf16)
            source[base + k] = tile
    tile_products(coords, pattern, source, acc, True)
    for out, half in ((keep, c), (send, 1 - c)):
        for r in range(4):
            base = half * (COL_TILES // 2) + (x ^ r) * OWN
            for k in range(OWN):
                out[r, tile_rows(k), :] = acc[base + k].astype(out.dtype)
            if first:
                counts = jnp.concatenate(
                    [sizes[pl.ds(pl.multiple_of(base, OWN), OWN), :], jnp.zeros((COUNT_ROWS - OWN, TILE), f32)], axis=0
                )
                out[r, CHUNK : CHUNK + COUNT_ROWS, :] = counts.astype(out.dtype)


def forward(first, place, coords, blocks, degrees, sizes, pattern):
    rows = CHUNK + (COUNT_ROWS if first else 0)
    outs = [shape(4, rows, TILE), shape(4, rows, TILE, dtype=bf16)]
    if first:
        outs.append(shape(ROW_TILES, TILE))
    args = [*blocks, *degrees, sizes, pattern] if first else [*blocks, pattern]
    return call(
        functools.partial(forward_kernel, first),
        "forward",
        tuple(outs),
        [SMEM, SMEM] + [VMEM] * len(args),
        scratch=[pltpu.VMEM((ROW_TILES, K, TILE), bf16), pltpu.VMEM((COL_TILES, K, TILE), f32)],
        limit=20,
        flops=6 * 10**9,
        moved=12 * MIB,
    )(place, coords, *args)


def halves_kernel(keep, arrived, own, s1, s2, s3):
    for r, out in enumerate((own, s1, s2, s3)):
        out[...] = (keep[r] + arrived[r].astype(f32)).astype(out.dtype)


def halves(keep, arrived):
    rows = keep.shape[1]
    outs = [shape(rows, TILE)] + [shape(rows, TILE, dtype=bf16)] * 3
    return call(halves_kernel, "halves", tuple(outs), [VMEM] * 2, moved=3 * MIB)(keep, arrived)


def total_kernel(own, r1, r2, r3, out):
    total = (own[...] + r1[...].astype(f32)) + (r2[...].astype(f32) + r3[...].astype(f32))
    out[...] = total.astype(bf16)


def weigh_kernel(first, *refs):
    if first:
        place, p0, p1, p2, p3, weight, weighted, scale = refs
    else:
        place, p0, p1, p2, p3, scale, factor, weighted = refs
    add = lambda at: (p0[at, :].astype(f32) + p1[at, :].astype(f32)) + (p2[at, :].astype(f32) + p3[at, :].astype(f32))
    if first:
        x, z, c, y, _ = place_of(place)
        base = pl.multiple_of(c * (COL_TILES // 2) + x * OWN, OWN)
        counts = add(slice(CHUNK, CHUNK + COUNT_ROWS))[:OWN]
        scale[...] = weight[pl.ds(base, OWN), :] / jnp.maximum(counts, 1.0)
    for k in range(OWN):
        tile = add(tile_rows(k))
        if not first:
            tile = jnp.dot(factor[...], tile, precision=HIGHEST, preferred_element_type=f32)
        weighted[tile_rows(k), :] = (tile * scale[k : k + 1, :]).astype(bf16)


def backward_kernel(place, coords, w0, w1, w2, w3, other, pattern, own, s1, s2, s3, source, acc):
    x, z, c, y, _ = place_of(place)
    for r, block in enumerate((w0, w1, w2, w3)):
        base = c * (COL_TILES // 2) + (x ^ r) * OWN
        far = (1 - c) * (COL_TILES // 2) + (x ^ r) * OWN
        for k in range(OWN):
            source[base + k] = block[tile_rows(k), :]
            source[far + k] = other[r, tile_rows(k), :]
    tile_products(coords, pattern, source, acc, False)
    for s, out in enumerate((own, s1, s2, s3)):
        base = (y ^ s) * OWN
        for k in range(OWN):
            out[tile_rows(k), :] = acc[base + k].astype(out.dtype)


def backward(place, coords, blocks, other, pattern):
    outs = [shape(CHUNK, TILE)] + [shape(CHUNK, TILE, dtype=bf16)] * 3
    return call(
        backward_kernel,
        "backward",
        tuple(outs),
        [SMEM, SMEM] + [VMEM] * 6,
        scratch=[pltpu.VMEM((COL_TILES, K, TILE), bf16), pltpu.VMEM((ROW_TILES, K, TILE), f32)],
        limit=20,
        flops=6 * 10**9,
        moved=12 * MIB,
    )(place, coords, *blocks, other, pattern)


def image_kernel(last, place, own, r1, r2, r3, inv, image, gram, *scaled):
    x, z, c, y, _ = place_of(place)
    inv_own = inv[pl.ds(pl.multiple_of(y * OWN, OWN), OWN), :]
    total = jnp.zeros((K, K), f32)
    for k in range(OWN):
        at = tile_rows(k)
        tile = (own[at, :] + r1[at, :].astype(f32)) + (r2[at, :].astype(f32) + r3[at, :].astype(f32))
        tile = tile * inv_own[k : k + 1, :]
        image[at, :] = tile
        if not last:
            scaled[0][at, :] = (tile * inv_own[k : k + 1, :]).astype(bf16)
        total += lax.dot_general(
            tile, tile, (((1,), (1,)), ((), ())), precision=HIGHEST, preferred_element_type=f32
        )
    gram[...] = total / TOTAL_DOCS


def inverse_factor_kernel(gram, out):
    work = jnp.concatenate([gram[...], jnp.eye(K, dtype=f32)], axis=1)
    rows = lax.broadcasted_iota(jnp.int32, (K, 1), 0)
    for k in range(K):
        pivot = work[k : k + 1, :]
        ratio = jnp.where(rows > k, work[:, k : k + 1] / pivot[:, k : k + 1], 0.0)
        work = work - ratio * pivot
    diagonal = lax.broadcasted_iota(jnp.int32, (K, K), 0) == lax.broadcasted_iota(jnp.int32, (K, K), 1)
    pivots = jnp.sum(jnp.where(diagonal, work[:, :K], 0.0), axis=1, keepdims=True)
    out[...] = work[:, K:] / jnp.sqrt(pivots)


def solve_kernel(factor, image, out):
    for k in range(OWN):
        out[:, k * TILE : (k + 1) * TILE] = jnp.dot(
            factor[...], image[tile_rows(k), :], precision=HIGHEST, preferred_element_type=f32
        )


def swapped(values, axis):
    return [swap(value, axis, s + 1) for s, value in enumerate(values)]


def body(start_vectors, bucket_weight, tile_count, tile_coords, patterns):
    place = jnp.stack([lax.axis_index(a) for a in DOC_BKT] + [tile_count[0, 0]]).astype(jnp.int32)
    coords = tile_coords.reshape(2 * SLOTS)
    weight = bucket_weight.reshape(COL_TILES, TILE)
    chunk = shape(CHUNK, TILE)
    chunk_b = shape(CHUNK, TILE, dtype=bf16)

    block = call(cast_kernel, "cast", chunk_b, [VMEM])(start_vectors)
    blocks = [block] + [swap(block, BKT, s) for s in (1, 2, 3)]
    pattern, doc_part, size_part = prep(place, coords, weight, patterns.reshape(SLOTS, TILE, TILE))
    degrees = [doc_part] + [swap(doc_part, BKT, s) for s in (1, 2, 3)]
    inv = scale = factor = None
    for sweep in range(ITERS):
        first, last = sweep == 0, sweep == ITERS - 1
        outs = forward(first, place, coords, blocks, degrees, size_part, pattern)
        if first:
            keep, send, inv = outs
        else:
            keep, send = outs
        own, *parts = halves(keep, swap(send, CORE, 1))
        parts = swapped(parts, X)
        part = call(total_kernel, "total", shape(*own.shape, dtype=bf16), [VMEM] * 4)(own, *parts)
        parts = [part] + [swap(part, Z, s) for s in (1, 2, 3)]
        if first:
            weighted, scale = call(
                functools.partial(weigh_kernel, True), "weigh", (chunk_b, shape(OWN, TILE)), [SMEM] + [VMEM] * 5
            )(place, *parts, weight)
        else:
            weighted = call(functools.partial(weigh_kernel, False), "weigh", chunk_b, [SMEM] + [VMEM] * 6)(
                place, *parts, scale, factor
            )
        mine = [weighted] + [swap(weighted, X, s) for s in (1, 2, 3)]
        other = swap(jnp.stack(mine), CORE, 1)
        own, *parts = backward(place, coords, mine, other, pattern)
        outs = (chunk, shape(K, K)) + (() if last else (chunk_b,))
        outs = call(functools.partial(image_kernel, last), "image", outs, [SMEM] + [VMEM] * 5)(
            place, own, *swapped(parts, BKT), inv
        )
        image, gram = outs[:2]
        if not last:
            blocks = [outs[2]] + [swap(outs[2], BKT, s) for s in (1, 2, 3)]
        for axis, mask in ((CORE, 1), (BKT, 1), (BKT, 3), (X, 1), (X, 3), (Z, 1), (Z, 3)):
            gram = gram + swap(gram, axis, mask)
        factor = call(inverse_factor_kernel, "inverse_factor", shape(K, K), [VMEM])(gram)
    return call(solve_kernel, "solve", shape(K, OWN * TILE), [VMEM] * 2)(factor, image)


def solution(mesh):
    split = Mesh(mesh.devices.reshape(4, 4, 2, mesh.shape[BKT]), DOC_BKT)
    in_specs = (
        P(None, DOC_BKT),
        P(BKT),
        P(DOC, BKT),
        P(DOC, BKT, None, None),
        P(DOC, BKT, None, None, None),
    )
    return jax.shard_map(body, mesh=split, in_specs=in_specs, out_specs=P(None, DOC_BKT), check_vma=False)
```

```python
import functools

import jax
import jax.numpy as jnp
from jax import lax
from jax.experimental import pallas as pl
from jax.experimental.pallas import tpu as pltpu
from jax.sharding import Mesh
from jax.sharding import PartitionSpec as P

ITERS = 2
K = 64
TILE = 128
SLOTS = 256
ROW_TILES = 32
COL_TILES = 64
TOTAL_DOCS = 131072
OWN = 8
CHUNK = OWN * K
COUNT_ROWS = 16
PACKED = 96
TURN = 16
PIVOTS = 8
UNROLL = 32
PREP_STEP = 32
MIB = 1 << 20
PREP_LIMIT = 32 * MIB

X, Z, CORE, BKT = "doc_0", "doc_1", "doc_2", "bkt"
DOC = (X, Z, CORE)
DOC_BKT = (X, Z, CORE, BKT)

f32 = jnp.float32
bf16 = jnp.bfloat16
SMEM = pl.BlockSpec(memory_space=pltpu.SMEM)
VMEM = pl.BlockSpec(memory_space=pltpu.VMEM)
HIGHEST = lax.Precision.HIGHEST


def shape(*lengths, dtype=f32):
    return jax.ShapeDtypeStruct(lengths, dtype)


def call(kernel, name, out_shape, in_specs, scratch=(), limit=8, flops=0, moved=0):
    return pl.pallas_call(
        kernel,
        out_shape=out_shape,
        in_specs=in_specs,
        out_specs=jax.tree.map(lambda _: VMEM, out_shape),
        scratch_shapes=list(scratch),
        compiler_params=pltpu.CompilerParams(vmem_limit_bytes=limit * MIB),
        cost_estimate=pl.CostEstimate(flops=flops, bytes_accessed=moved, transcendentals=0),
        name=name,
    )


def swap(value, axis, mask):
    size = lax.axis_size(axis)
    return lax.ppermute(value, axis, [(i, i ^ mask) for i in range(size)])


def place_of(place):
    return place[0], place[1], place[2], place[3], place[4]


def tile_rows(k):
    return slice(k * K, (k + 1) * K)


def split3(value):
    high = value.astype(bf16)
    rest = value - high.astype(f32)
    middle = rest.astype(bf16)
    return high, middle, (rest - middle.astype(f32)).astype(bf16)


def pack_gram(gram):
    high, middle, low = (term.astype(f32) for term in split3(gram))
    top = jnp.concatenate([high, middle], axis=1)
    bottom = jnp.concatenate([low[: K // 2], low[K // 2 :]], axis=1)
    return jnp.concatenate([top, bottom], axis=0).astype(bf16)


def unpack_gram(packed):
    packed = packed.astype(f32)
    low = jnp.concatenate([packed[K:, :K], packed[K:, K:]], axis=0)
    return (packed[:K, :K] + packed[:K, K:]) + low


def prep_kernel(
    place, coords, weight, pattern_hbm,
    pattern, doc_part, size_part,
    raw, split, doc_acc, size_acc, sems,
):
    steps = SLOTS // PREP_STEP

    def fetch(step):
        at = pl.ds(step * PREP_STEP, PREP_STEP)
        return pltpu.make_async_copy(pattern_hbm.at[at], raw.at[at], sems.at[step])

    for step in range(steps):
        fetch(step).start()
    doc_acc[...] = jnp.zeros_like(doc_acc)
    size_acc[...] = jnp.zeros_like(size_acc)
    rows = lax.broadcasted_iota(jnp.int32, split.shape, 1)
    terms = jnp.zeros(split.shape, f32)
    for i, term in enumerate(split3(weight[...])):
        terms = jnp.where(rows == i, jnp.broadcast_to(term.astype(f32)[:, None, :], split.shape), terms)
    split[...] = terms.astype(bf16)
    count = place[4]

    def block(step, carry):
        fetch(step).wait()
        products, sums = [], []
        for u in range(PREP_STEP):
            slot = step * PREP_STEP + u
            tile = jnp.where(slot < count, raw[slot], 0).astype(f32)
            sums.append(jnp.sum(tile.reshape(TILE // 8, 8, TILE), axis=0))
            tile = tile.astype(bf16)
            pattern[slot] = tile
            products.append(
                lax.dot_general(
                    split[coords[2 * slot + 1]], tile, (((1,), (1,)), ((), ())), preferred_element_type=f32
                )
            )
        for u in range(PREP_STEP):
            slot = step * PREP_STEP + u
            doc_acc[coords[2 * slot]] += products[u]
            size_acc[coords[2 * slot + 1]] += sums[u]
        return carry

    lax.fori_loop(0, steps, block, 0)
    doc_part[...] = jnp.sum(doc_acc[...], axis=1)
    size_part[...] = jnp.sum(size_acc[...], axis=1)


def pack_kernel(vectors, doc_part, payload):
    for k in range(OWN):
        payload[tile_rows(k), :] = vectors[:, k * TILE : (k + 1) * TILE].astype(bf16)
    for i, term in enumerate(split3(doc_part[...])):
        payload[CHUNK + i * ROW_TILES : CHUNK + (i + 1) * ROW_TILES, :] = term


def prep(place, coords, weight, patterns):
    return pl.pallas_call(
        prep_kernel,
        out_shape=(
            shape(SLOTS, TILE, TILE, dtype=bf16),
            shape(ROW_TILES, TILE),
            shape(COL_TILES, TILE),
        ),
        in_specs=[SMEM, SMEM, VMEM, pl.BlockSpec(memory_space=pltpu.HBM)],
        out_specs=(VMEM, VMEM, VMEM),
        scratch_shapes=[
            pltpu.VMEM((SLOTS, TILE, TILE), jnp.int32),
            pltpu.VMEM((COL_TILES, 16, TILE), bf16),
            pltpu.VMEM((ROW_TILES, 16, TILE), f32),
            pltpu.VMEM((COL_TILES, 8, TILE), f32),
            pltpu.SemaphoreType.DMA((SLOTS // PREP_STEP,)),
        ],
        compiler_params=pltpu.CompilerParams(vmem_limit_bytes=PREP_LIMIT),
        cost_estimate=pl.CostEstimate(flops=10**9, bytes_accessed=24 * MIB, transcendentals=0),
        name="prep",
    )(place, coords, weight, patterns)


def turn_kernel(pattern, turned):
    def group(g, carry):
        for u in range(TURN):
            slot = g * TURN + u
            turned[slot] = pattern[slot].T
        return carry

    lax.fori_loop(0, SLOTS // TURN, group, 0)


def tile_products(coords, pattern, source, acc, read, write):
    acc[...] = jnp.zeros_like(acc)

    def group(g, carry):
        products = []
        for u in range(UNROLL):
            slot = g * UNROLL + u
            products.append(
                jnp.dot(source[coords[2 * slot + read]], pattern[slot], preferred_element_type=f32)
            )
        for u in range(UNROLL):
            slot = g * UNROLL + u
            acc[coords[2 * slot + write]] += products[u]
        return carry

    lax.fori_loop(0, SLOTS // UNROLL, group, 0)


def forward_kernel(first, place, coords, b0, b1, b2, b3, pattern, *refs):
    if first:
        sizes, _, keep, send, inv, source, acc = refs
    else:
        keep, send, gram, source, acc = refs
    x, z, c, y, _ = place_of(place)
    blocks = (b0, b1, b2, b3)
    if first:
        terms = [block[CHUNK + i * ROW_TILES : CHUNK + (i + 1) * ROW_TILES, :].astype(f32) for block in blocks for i in range(3)]
        parts = [(terms[3 * s] + terms[3 * s + 1]) + terms[3 * s + 2] for s in range(4)]
        inv[...] = 1.0 / jnp.sqrt(jnp.maximum((parts[0] + parts[1]) + (parts[2] + parts[3]), 1.0))
    for s, block in enumerate(blocks):
        base = (y ^ s) * OWN
        for k in range(OWN):
            tile = block[tile_rows(k), :]
            if first:
                tile = (tile.astype(f32) * inv[pl.ds(base + k, 1), :]).astype(bf16)
            source[base + k] = tile
    tile_products(coords, pattern, source, acc, 0, 1)
    for out, half in ((keep, c), (send, 1 - c)):
        for r in range(4):
            base = half * (COL_TILES // 2) + (x ^ r) * OWN
            for k in range(OWN):
                at = r * CHUNK + k * K
                out[at : at + K, :] = acc[base + k].astype(out.dtype)
            if first:
                counts = jnp.concatenate(
                    [sizes[pl.ds(pl.multiple_of(base, OWN), OWN), :], jnp.zeros((COUNT_ROWS - OWN, TILE), f32)], axis=0
                )
                at = 4 * CHUNK + r * COUNT_ROWS
                out[at : at + COUNT_ROWS, :] = counts.astype(out.dtype)
    if not first:
        parts = [unpack_gram(block[CHUNK : CHUNK + PACKED, :]) for block in blocks]
        gram[...] = (parts[0] + parts[1]) + (parts[2] + parts[3])
        send[4 * CHUNK : 4 * CHUNK + PACKED, :] = pack_gram(gram[...])


def forward(first, place, coords, blocks, pattern, *sizes):
    extra = 4 * COUNT_ROWS
    outs = (
        shape(4 * CHUNK + (extra if first else 0), TILE),
        shape(4 * CHUNK + (extra if first else PACKED), TILE, dtype=bf16),
        shape(ROW_TILES, TILE) if first else shape(K, K),
    )
    return call(
        functools.partial(forward_kernel, first),
        "forward",
        outs,
        [SMEM, SMEM] + [VMEM] * (5 + len(sizes)),
        scratch=[pltpu.VMEM((ROW_TILES, K, TILE), bf16), pltpu.VMEM((COL_TILES, K, TILE), f32)],
        limit=20,
        flops=6 * 10**9,
        moved=12 * MIB,
    )(place, coords, *blocks, pattern, *sizes)


def halves_kernel(first, *refs):
    if first:
        keep, arrived, own, s1, s2, s3 = refs
    else:
        keep, gram, arrived, own, s1, s2, s3, gram_out = refs
        gram_out[...] = gram[...] + unpack_gram(arrived[4 * CHUNK : 4 * CHUNK + PACKED, :])
        packed = pack_gram(gram_out[...])
    for r, out in enumerate((own, s1, s2, s3)):
        at = slice(r * CHUNK, (r + 1) * CHUNK)
        out[:CHUNK, :] = (keep[at, :] + arrived[at, :].astype(f32)).astype(out.dtype)
        if first:
            at = slice(4 * CHUNK + r * COUNT_ROWS, 4 * CHUNK + (r + 1) * COUNT_ROWS)
            out[CHUNK:, :] = (keep[at, :] + arrived[at, :].astype(f32)).astype(out.dtype)
        elif r:
            out[CHUNK:, :] = packed


def halves(first, *args):
    rows = CHUNK + (COUNT_ROWS if first else PACKED)
    outs = [shape(rows if first else CHUNK, TILE)] + [shape(rows, TILE, dtype=bf16)] * 3
    if not first:
        outs.append(shape(K, K))
    return call(functools.partial(halves_kernel, first), "halves", tuple(outs), [VMEM] * len(args), moved=3 * MIB)(*args)


def add4(own, r1, r2, r3, at):
    return (own[at, :].astype(f32) + r1[at, :].astype(f32)) + (r2[at, :].astype(f32) + r3[at, :].astype(f32))


def add_grams(gram, *refs):
    parts = [unpack_gram(ref[CHUNK : CHUNK + PACKED, :]) for ref in refs]
    return (gram[...] + parts[0]) + (parts[1] + parts[2])


def total_kernel(first, *refs):
    if first:
        own, r1, r2, r3, out = refs
        out[...] = add4(own, r1, r2, r3, slice(None)).astype(bf16)
    else:
        own, r1, r2, r3, gram, out, gram_out = refs
        out[:CHUNK, :] = add4(own, r1, r2, r3, slice(0, CHUNK)).astype(bf16)
        gram_out[...] = add_grams(gram, r1, r2, r3)
        out[CHUNK:, :] = pack_gram(gram_out[...])


def total(first, *args):
    rows = CHUNK + (COUNT_ROWS if first else PACKED)
    outs = (shape(rows, TILE, dtype=bf16),) + (() if first else (shape(K, K),))
    return call(functools.partial(total_kernel, first), "total", outs, [VMEM] * len(args))(*args)


def inverse_factor(gram):
    work = jnp.concatenate([gram, jnp.eye(K, dtype=f32)], axis=1)
    below = lax.broadcasted_iota(jnp.int32, (K, 1), 0)
    for k in range(0, K, PIVOTS):
        cols = [jnp.broadcast_to(work[:, k + j : k + j + 1], (K, 2 * K)) for j in range(PIVOTS)]
        rows = [work[k + j : k + j + 1, :] for j in range(PIVOTS)]
        for j in range(PIVOTS):
            inverse = 1.0 / cols[j][k + j : k + j + 1, :]
            row = rows[j] * inverse
            for i in range(j + 1, PIVOTS):
                factor = cols[j][k + i : k + i + 1, :]
                rows[i] = rows[i] - factor * row
                cols[i] = cols[i] - cols[j] * (factor * inverse)
            work = work - jnp.where(below > k + j, cols[j], 0.0) * row
    diagonal = lax.broadcasted_iota(jnp.int32, (K, K), 0) == lax.broadcasted_iota(jnp.int32, (K, K), 1)
    pivots = jnp.sum(jnp.where(diagonal, work[:, :K], 0.0), axis=1, keepdims=True)
    return work[:, K:] / jnp.sqrt(pivots)


def weigh_kernel(first, *refs):
    if first:
        place, p0, p1, p2, p3, weight, weighted, scale = refs
        x, z, c, y, _ = place_of(place)
        base = pl.multiple_of(c * (COL_TILES // 2) + x * OWN, OWN)
        counts = add4(p0, p1, p2, p3, slice(CHUNK, CHUNK + COUNT_ROWS))[:OWN]
        scale[...] = weight[pl.ds(base, OWN), :] / jnp.maximum(counts, 1.0)
    else:
        p0, p1, p2, p3, gram, scale, weighted = refs
        factor = inverse_factor(add_grams(gram, p1, p2, p3))
    for k in range(OWN):
        tile = add4(p0, p1, p2, p3, tile_rows(k))
        if not first:
            tile = jnp.dot(factor, tile, precision=HIGHEST, preferred_element_type=f32)
        weighted[tile_rows(k), :] = (tile * scale[k : k + 1, :]).astype(bf16)


def backward_kernel(place, coords, w0, w1, w2, w3, other, turned, own, s1, s2, s3, source, acc):
    x, z, c, y, _ = place_of(place)
    for r, block in enumerate((w0, w1, w2, w3)):
        base = c * (COL_TILES // 2) + (x ^ r) * OWN
        far = (1 - c) * (COL_TILES // 2) + (x ^ r) * OWN
        for k in range(OWN):
            source[base + k] = block[tile_rows(k), :]
            source[far + k] = other[r, tile_rows(k), :]
    tile_products(coords, turned, source, acc, 1, 0)
    for s, out in enumerate((own, s1, s2, s3)):
        base = (y ^ s) * OWN
        for k in range(OWN):
            out[tile_rows(k), :] = acc[base + k].astype(out.dtype)


def backward(place, coords, blocks, other, turned):
    outs = [shape(CHUNK, TILE)] + [shape(CHUNK, TILE, dtype=bf16)] * 3
    return call(
        backward_kernel,
        "backward",
        tuple(outs),
        [SMEM, SMEM] + [VMEM] * 6,
        scratch=[pltpu.VMEM((COL_TILES, K, TILE), bf16), pltpu.VMEM((ROW_TILES, K, TILE), f32)],
        limit=20,
        flops=6 * 10**9,
        moved=12 * MIB,
    )(place, coords, *blocks, other, turned)


def image_kernel(last, place, own, r1, r2, r3, inv, *refs):
    x, z, c, y, _ = place_of(place)
    inv_own = inv[pl.ds(pl.multiple_of(y * OWN, OWN), OWN), :]
    gram = jnp.zeros((K, K), f32)
    for k in range(OWN):
        at = tile_rows(k)
        tile = add4(own, r1, r2, r3, at) * inv_own[k : k + 1, :]
        if last:
            refs[0][at, :] = tile
        else:
            refs[0][at, :] = (tile * inv_own[k : k + 1, :]).astype(bf16)
        gram += lax.dot_general(
            tile, tile, (((1,), (1,)), ((), ())), precision=HIGHEST, preferred_element_type=f32
        )
    gram = gram / TOTAL_DOCS
    if last:
        image, keep, send, whole = refs
        whole[...] = gram
        for out, half in ((keep, c), (send, 1 - c)):
            rows = whole[pl.ds(pl.multiple_of(half * (K // 2), K // 2), K // 2), :]
            out[...] = jnp.concatenate([rows[: K // 4], rows[K // 4 :]], axis=1)
    else:
        refs[0][CHUNK:, :] = pack_gram(gram)


def sum_kernel(parts, out):
    out[...] = jnp.sum(parts[...], axis=0)


def solve_kernel(place, half, other, image, out, whole):
    c = place[2]
    for ref, at in ((half, c), (other, 1 - c)):
        rows = jnp.concatenate([ref[:, :K], ref[:, K:]], axis=0)
        whole[pl.ds(pl.multiple_of(at * (K // 2), K // 2), K // 2), :] = rows
    factor = inverse_factor(whole[...])
    for k in range(OWN):
        out[:, k * TILE : (k + 1) * TILE] = jnp.dot(
            factor, image[tile_rows(k), :], precision=HIGHEST, preferred_element_type=f32
        )


def spread(value, axis):
    return [value] + [swap(value, axis, s) for s in (1, 2, 3)]


def swapped(values, axis):
    return [swap(value, axis, s + 1) for s, value in enumerate(values)]


def body(start_vectors, bucket_weight, tile_count, tile_coords, patterns):
    place = jnp.stack([lax.axis_index(a) for a in DOC_BKT] + [tile_count[0, 0]]).astype(jnp.int32)
    coords = tile_coords.reshape(2 * SLOTS)
    weight = bucket_weight.reshape(COL_TILES, TILE)
    chunk_b = shape(CHUNK, TILE, dtype=bf16)

    pattern, doc_part, sizes = prep(place, coords, weight, patterns.reshape(SLOTS, TILE, TILE))
    payload = call(pack_kernel, "pack", shape(CHUNK + PACKED, TILE, dtype=bf16), [VMEM] * 2)(start_vectors, doc_part)
    turned = call(turn_kernel, "turn", shape(SLOTS, TILE, TILE, dtype=bf16), [VMEM], limit=4, moved=16 * MIB)(pattern)
    inv = scale = None
    for sweep in range(ITERS):
        first, last = sweep == 0, sweep == ITERS - 1
        blocks = spread(payload, BKT)
        if first:
            keep, send, inv = forward(True, place, coords, blocks, pattern, sizes, turned)
            own, *parts = halves(True, keep, swap(send, CORE, 1))
            (part,) = total(True, own, *swapped(parts, X))
            weighted, scale = call(
                functools.partial(weigh_kernel, True), "weigh", (chunk_b, shape(OWN, TILE)), [SMEM] + [VMEM] * 5
            )(place, *spread(part, Z), weight)
        else:
            keep, send, gram = forward(False, place, coords, blocks, pattern)
            own, *parts, gram = halves(False, keep, gram, swap(send, CORE, 1))
            part, gram = total(False, own, *swapped(parts, X), gram)
            weighted = call(functools.partial(weigh_kernel, False), "weigh", chunk_b, [VMEM] * 6)(
                *spread(part, Z), gram, scale
            )
        mine = spread(weighted, X)
        other = swap(jnp.stack(mine), CORE, 1)
        own, *parts = backward(place, coords, mine, other, turned)
        if not last:
            outs = shape(CHUNK + PACKED, TILE, dtype=bf16)
            scratch = ()
        else:
            outs = (shape(CHUNK, TILE), shape(K // 4, TILE), shape(K // 4, TILE))
            scratch = (pltpu.VMEM((K, K), f32),)
        outs = call(functools.partial(image_kernel, last), "image", outs, [SMEM] + [VMEM] * 5, scratch=scratch)(
            place, own, *swapped(parts, BKT), inv
        )
        if not last:
            payload = outs
    image, keep, send = outs
    half = keep + swap(send, CORE, 1)
    others = (X, Z, BKT)
    copies = jnp.broadcast_to(half, (lax.axis_size(others), *half.shape))
    parts = lax.all_to_all(copies, others, split_axis=0, concat_axis=0, tiled=True)
    half = call(sum_kernel, "sum", shape(K // 4, TILE), [VMEM])(parts)
    return call(
        solve_kernel,
        "solve",
        shape(K, OWN * TILE),
        [SMEM] + [VMEM] * 3,
        scratch=[pltpu.VMEM((K, K), f32)],
    )(place, half, swap(half, CORE, 1), image)


def solution(mesh):
    split = Mesh(mesh.devices.reshape(4, 4, 2, mesh.shape[BKT]), DOC_BKT)
    in_specs = (
        P(None, DOC_BKT),
        P(BKT),
        P(DOC, BKT),
        P(DOC, BKT, None, None),
        P(DOC, BKT, None, None, None),
    )
    return jax.shard_map(body, mesh=split, in_specs=in_specs, out_specs=P(None, DOC_BKT), check_vma=False)
```

```python
import functools

import jax
import jax.numpy as jnp
from jax import lax
from jax.experimental import pallas as pl
from jax.experimental.pallas import tpu as pltpu
from jax.sharding import Mesh
from jax.sharding import PartitionSpec as P

ITERS = 2
K = 64
TILE = 128
SLOTS = 256
ROW_TILES = 32
COL_TILES = 64
TOTAL_DOCS = 131072
OWN = 8
CHUNK = OWN * K
COUNT_ROWS = 16
PACKED = 96
TURN = 32
SEND = (1, 2, 3)
PIVOTS = 8
UNROLL = 128
PREP_STEP = 32
MIB = 1 << 20
PREP_LIMIT = 32 * MIB

X, Z, CORE, BKT = "doc_0", "doc_1", "doc_2", "bkt"
DOC = (X, Z, CORE)
DOC_BKT = (X, Z, CORE, BKT)

f32 = jnp.float32
bf16 = jnp.bfloat16
SMEM = pl.BlockSpec(memory_space=pltpu.SMEM)
VMEM = pl.BlockSpec(memory_space=pltpu.VMEM)
HIGHEST = lax.Precision.HIGHEST


def shape(*lengths, dtype=f32):
    return jax.ShapeDtypeStruct(lengths, dtype)


def call(kernel, name, out_shape, in_specs, scratch=(), limit=8, flops=0, moved=0):
    return pl.pallas_call(
        kernel,
        out_shape=out_shape,
        in_specs=in_specs,
        out_specs=jax.tree.map(lambda _: VMEM, out_shape),
        scratch_shapes=list(scratch),
        compiler_params=pltpu.CompilerParams(vmem_limit_bytes=limit * MIB),
        cost_estimate=pl.CostEstimate(flops=flops, bytes_accessed=moved, transcendentals=0),
        name=name,
    )


def swap(value, axis, mask):
    size = lax.axis_size(axis)
    return lax.ppermute(value, axis, [(i, i ^ mask) for i in range(size)])


def place_of(place):
    return place[0], place[1], place[2], place[3], place[4]


def tile_rows(k):
    return slice(k * K, (k + 1) * K)


def split3(value):
    high = value.astype(bf16)
    rest = value - high.astype(f32)
    middle = rest.astype(bf16)
    return high, middle, (rest - middle.astype(f32)).astype(bf16)


def times(factor, value):
    f_high, f_low, _ = split3(factor)
    v_high, v_low, _ = split3(value)
    both = jnp.dot(jnp.concatenate([f_high, f_low], axis=0), v_high, preferred_element_type=f32)
    low = jnp.dot(f_high, v_low, preferred_element_type=f32)
    return both[:K] + (both[K:] + low)


def pack_gram(gram):
    high, middle, low = (term.astype(f32) for term in split3(gram))
    top = jnp.concatenate([high, middle], axis=1)
    bottom = jnp.concatenate([low[: K // 2], low[K // 2 :]], axis=1)
    return jnp.concatenate([top, bottom], axis=0).astype(bf16)


def unpack_gram(packed):
    packed = packed.astype(f32)
    low = jnp.concatenate([packed[K:, :K], packed[K:, K:]], axis=0)
    return (packed[:K, :K] + packed[:K, K:]) + low


def prep_kernel(
    place, coords, weight, pattern_hbm,
    pattern, doc_part, size_part,
    raw, split, doc_acc, size_acc, sems,
):
    steps = SLOTS // PREP_STEP

    def fetch(step):
        at = pl.ds(step * PREP_STEP, PREP_STEP)
        return pltpu.make_async_copy(pattern_hbm.at[at], raw.at[at], sems.at[step])

    for step in range(steps):
        fetch(step).start()
    doc_acc[...] = jnp.zeros_like(doc_acc)
    size_acc[...] = jnp.zeros_like(size_acc)
    rows = lax.broadcasted_iota(jnp.int32, split.shape, 1)
    terms = jnp.zeros(split.shape, f32)
    for i, term in enumerate(split3(weight[...])):
        terms = jnp.where(rows == i, jnp.broadcast_to(term.astype(f32)[:, None, :], split.shape), terms)
    split[...] = terms.astype(bf16)
    count = place[4]

    def block(step, carry):
        fetch(step).wait()
        products, sums = [], []
        for u in range(PREP_STEP):
            slot = step * PREP_STEP + u
            tile = jnp.where(slot < count, raw[slot], 0).astype(f32)
            sums.append(jnp.sum(tile.reshape(TILE // 8, 8, TILE), axis=0))
            tile = tile.astype(bf16)
            pattern[slot] = tile
            products.append(
                lax.dot_general(
                    split[coords[2 * slot + 1]], tile, (((1,), (1,)), ((), ())), preferred_element_type=f32
                )
            )
        for u in range(PREP_STEP):
            slot = step * PREP_STEP + u
            doc_acc[coords[2 * slot]] += products[u]
            size_acc[coords[2 * slot + 1]] += sums[u]
        return carry

    lax.fori_loop(0, steps, block, 0)
    doc_part[...] = jnp.sum(doc_acc[...], axis=1)
    size_part[...] = jnp.sum(size_acc[...], axis=1)


def pack_kernel(vectors, doc_part, payload):
    for k in range(OWN):
        payload[tile_rows(k), :] = vectors[:, k * TILE : (k + 1) * TILE].astype(bf16)
    for i, term in enumerate(split3(doc_part[...])):
        payload[CHUNK + i * ROW_TILES : CHUNK + (i + 1) * ROW_TILES, :] = term


def prep(place, coords, weight, patterns):
    return pl.pallas_call(
        prep_kernel,
        out_shape=(
            shape(SLOTS, TILE, TILE, dtype=bf16),
            shape(ROW_TILES, TILE),
            shape(COL_TILES, TILE),
        ),
        in_specs=[SMEM, SMEM, VMEM, pl.BlockSpec(memory_space=pltpu.HBM)],
        out_specs=(VMEM, VMEM, VMEM),
        scratch_shapes=[
            pltpu.VMEM((SLOTS, TILE, TILE), jnp.int32),
            pltpu.VMEM((COL_TILES, 16, TILE), bf16),
            pltpu.VMEM((ROW_TILES, 16, TILE), f32),
            pltpu.VMEM((COL_TILES, 8, TILE), f32),
            pltpu.SemaphoreType.DMA((SLOTS // PREP_STEP,)),
        ],
        compiler_params=pltpu.CompilerParams(vmem_limit_bytes=PREP_LIMIT),
        cost_estimate=pl.CostEstimate(flops=10**9, bytes_accessed=24 * MIB, transcendentals=0),
        name="prep",
    )(place, coords, weight, patterns)


def turn_kernel(pattern, turned):
    def group(g, carry):
        for u in range(TURN):
            slot = g * TURN + u
            turned[slot] = pattern[slot].T
        return carry

    lax.fori_loop(0, SLOTS // TURN, group, 0)


def tile_products(coords, pattern, source, acc, read, write):
    acc[...] = jnp.zeros_like(acc)

    def group(g, carry):
        products = []
        for u in range(UNROLL):
            slot = g * UNROLL + u
            products.append(
                jnp.dot(source[coords[2 * slot + read]], pattern[slot], preferred_element_type=f32)
            )
        for u in range(UNROLL):
            slot = g * UNROLL + u
            acc[coords[2 * slot + write]] += products[u]
        return carry

    lax.fori_loop(0, SLOTS // UNROLL, group, 0)


def forward_kernel(first, place, coords, b0, b1, b2, b3, pattern, *refs):
    if first:
        sizes, _, keep, send, inv, source, acc = refs
    else:
        keep, send, gram, source, acc = refs
    x, z, c, y, _ = place_of(place)
    blocks = (b0, b1, b2, b3)
    if first:
        terms = [block[CHUNK + i * ROW_TILES : CHUNK + (i + 1) * ROW_TILES, :].astype(f32) for block in blocks for i in range(3)]
        parts = [(terms[3 * s] + terms[3 * s + 1]) + terms[3 * s + 2] for s in range(4)]
        inv[...] = 1.0 / jnp.sqrt(jnp.maximum((parts[0] + parts[1]) + (parts[2] + parts[3]), 1.0))
    for s, block in enumerate(blocks):
        base = (y ^ s) * OWN
        for k in range(OWN):
            tile = block[tile_rows(k), :]
            if first:
                tile = (tile.astype(f32) * inv[pl.ds(base + k, 1), :]).astype(bf16)
            source[base + k] = tile
    tile_products(coords, pattern, source, acc, 0, 1)
    for out, half in ((keep, c), (send, 1 - c)):
        for r in range(4):
            base = half * (COL_TILES // 2) + (x ^ r) * OWN
            for k in range(OWN):
                at = r * CHUNK + k * K
                out[at : at + K, :] = acc[base + k].astype(out.dtype)
            if first:
                counts = jnp.concatenate(
                    [sizes[pl.ds(pl.multiple_of(base, OWN), OWN), :], jnp.zeros((COUNT_ROWS - OWN, TILE), f32)], axis=0
                )
                at = 4 * CHUNK + r * COUNT_ROWS
                out[at : at + COUNT_ROWS, :] = counts.astype(out.dtype)
    if not first:
        parts = [unpack_gram(block[CHUNK : CHUNK + PACKED, :]) for block in blocks]
        gram[...] = (parts[0] + parts[1]) + (parts[2] + parts[3])
        send[4 * CHUNK : 4 * CHUNK + PACKED, :] = pack_gram(gram[...])


def forward(first, place, coords, blocks, pattern, *sizes):
    extra = 4 * COUNT_ROWS
    outs = (
        shape(4 * CHUNK + (extra if first else 0), TILE),
        shape(4 * CHUNK + (extra if first else PACKED), TILE, dtype=bf16),
        shape(ROW_TILES, TILE) if first else shape(K, K),
    )
    return call(
        functools.partial(forward_kernel, first),
        "forward",
        outs,
        [SMEM, SMEM] + [VMEM] * (5 + len(sizes)),
        scratch=[pltpu.VMEM((ROW_TILES, K, TILE), bf16), pltpu.VMEM((COL_TILES, K, TILE), f32)],
        limit=20,
        flops=6 * 10**9,
        moved=12 * MIB,
    )(place, coords, *blocks, pattern, *sizes)


def halves_kernel(first, *refs):
    if first:
        keep, arrived, own, *sent = refs
    else:
        keep, gram, arrived, own, *sent, gram_out = refs
        gram_out[...] = gram[...] + unpack_gram(arrived[4 * CHUNK : 4 * CHUNK + PACKED, :])
        packed = pack_gram(gram_out[...])
    for r, out in ((0, own), *zip(SEND, sent)):
        at = slice(r * CHUNK, (r + 1) * CHUNK)
        out[:CHUNK, :] = (keep[at, :] + arrived[at, :].astype(f32)).astype(out.dtype)
        if first:
            at = slice(4 * CHUNK + r * COUNT_ROWS, 4 * CHUNK + (r + 1) * COUNT_ROWS)
            out[CHUNK:, :] = (keep[at, :] + arrived[at, :].astype(f32)).astype(out.dtype)
        elif r:
            out[CHUNK:, :] = packed


def halves(first, *args):
    rows = CHUNK + (COUNT_ROWS if first else PACKED)
    outs = [shape(rows if first else CHUNK, TILE)] + [shape(rows, TILE, dtype=bf16)] * 3
    if not first:
        outs.append(shape(K, K))
    return call(functools.partial(halves_kernel, first), "halves", tuple(outs), [VMEM] * len(args), moved=3 * MIB)(*args)


def add4(own, r1, r2, r3, at):
    return (own[at, :].astype(f32) + r1[at, :].astype(f32)) + (r2[at, :].astype(f32) + r3[at, :].astype(f32))


def add_grams(gram, *refs):
    parts = [unpack_gram(ref[CHUNK : CHUNK + PACKED, :]) for ref in refs]
    return (gram[...] + parts[0]) + (parts[1] + parts[2])


def total_kernel(first, *refs):
    if first:
        own, r1, r2, r3, out = refs
        out[...] = add4(own, r1, r2, r3, slice(None)).astype(bf16)
    else:
        own, r1, r2, r3, gram, out, gram_out = refs
        out[:CHUNK, :] = add4(own, r1, r2, r3, slice(0, CHUNK)).astype(bf16)
        gram_out[...] = add_grams(gram, r1, r2, r3)
        out[CHUNK:, :] = pack_gram(gram_out[...])


def total(first, *args):
    rows = CHUNK + (COUNT_ROWS if first else PACKED)
    outs = (shape(rows, TILE, dtype=bf16),) + (() if first else (shape(K, K),))
    return call(functools.partial(total_kernel, first), "total", outs, [VMEM] * len(args))(*args)


def inverse_factor(gram):
    work = jnp.concatenate([gram, jnp.eye(K, dtype=f32)], axis=1)
    below = lax.broadcasted_iota(jnp.int32, (K, 1), 0)
    for k in range(0, K, PIVOTS):
        cols = [jnp.broadcast_to(work[:, k + j : k + j + 1], (K, 2 * K)) for j in range(PIVOTS)]
        rows = [work[k + j : k + j + 1, :] for j in range(PIVOTS)]
        for j in range(PIVOTS):
            inverse = 1.0 / cols[j][k + j : k + j + 1, :]
            row = rows[j] * inverse
            for i in range(j + 1, PIVOTS):
                factor = cols[j][k + i : k + i + 1, :]
                rows[i] = rows[i] - factor * row
                cols[i] = cols[i] - cols[j] * (factor * inverse)
            work = work - jnp.where(below > k + j, cols[j], 0.0) * row
    diagonal = lax.broadcasted_iota(jnp.int32, (K, K), 0) == lax.broadcasted_iota(jnp.int32, (K, K), 1)
    pivots = jnp.sum(jnp.where(diagonal, work[:, :K], 0.0), axis=1, keepdims=True)
    return work[:, K:] / jnp.sqrt(pivots)


def weigh_kernel(first, *refs):
    if first:
        place, p0, p1, p2, p3, weight, weighted, scale = refs
        x, z, c, y, _ = place_of(place)
        base = pl.multiple_of(c * (COL_TILES // 2) + x * OWN, OWN)
        counts = add4(p0, p1, p2, p3, slice(CHUNK, CHUNK + COUNT_ROWS))[:OWN]
        scale[...] = weight[pl.ds(base, OWN), :] / jnp.maximum(counts, 1.0)
    else:
        p0, p1, p2, p3, gram, scale, weighted = refs
        factor = inverse_factor(add_grams(gram, p1, p2, p3))
    for k in range(OWN):
        tile = add4(p0, p1, p2, p3, tile_rows(k))
        if not first:
            tile = times(factor, tile)
        weighted[tile_rows(k), :] = (tile * scale[k : k + 1, :]).astype(bf16)


def backward_kernel(place, coords, w0, w1, w2, w3, other, turned, own, s1, s2, s3, source, acc):
    sent = (s1, s2, s3)
    x, z, c, y, _ = place_of(place)
    for r, block in enumerate((w0, w1, w2, w3)):
        base = c * (COL_TILES // 2) + (x ^ r) * OWN
        far = (1 - c) * (COL_TILES // 2) + (x ^ r) * OWN
        for k in range(OWN):
            source[base + k] = block[tile_rows(k), :]
            source[far + k] = other[r, tile_rows(k), :]
    tile_products(coords, turned, source, acc, 1, 0)
    for s, out in ((0, own), *zip(SEND, sent)):
        base = (y ^ s) * OWN
        for k in range(OWN):
            out[tile_rows(k), :] = acc[base + k].astype(out.dtype)


def backward(place, coords, blocks, other, turned):
    outs = [shape(CHUNK, TILE)] + [shape(CHUNK, TILE, dtype=bf16)] * 3
    return call(
        backward_kernel,
        "backward",
        tuple(outs),
        [SMEM, SMEM] + [VMEM] * 6,
        scratch=[pltpu.VMEM((COL_TILES, K, TILE), bf16), pltpu.VMEM((ROW_TILES, K, TILE), f32)],
        limit=20,
        flops=6 * 10**9,
        moved=12 * MIB,
    )(place, coords, *blocks, other, turned)


def image_kernel(last, place, own, r1, r2, r3, inv, *refs):
    x, z, c, y, _ = place_of(place)
    inv_own = inv[pl.ds(pl.multiple_of(y * OWN, OWN), OWN), :]
    gram = jnp.zeros((K, K), f32)
    for k in range(OWN):
        at = tile_rows(k)
        tile = add4(own, r1, r2, r3, at) * inv_own[k : k + 1, :]
        if last:
            refs[0][at, :] = tile
        else:
            refs[0][at, :] = (tile * inv_own[k : k + 1, :]).astype(bf16)
        gram += lax.dot_general(
            tile, tile, (((1,), (1,)), ((), ())), precision=HIGHEST, preferred_element_type=f32
        )
    gram = gram / TOTAL_DOCS
    if last:
        image, keep, send, whole = refs
        whole[...] = gram
        for out, half in ((keep, c), (send, 1 - c)):
            rows = whole[pl.ds(pl.multiple_of(half * (K // 2), K // 2), K // 2), :]
            out[...] = jnp.concatenate([rows[: K // 4], rows[K // 4 :]], axis=1)
    else:
        refs[0][CHUNK:, :] = pack_gram(gram)


def sum_kernel(parts, out):
    out[...] = jnp.sum(parts[...], axis=0)


def solve_kernel(place, half, other, image, out, whole):
    c = place[2]
    for ref, at in ((half, c), (other, 1 - c)):
        rows = jnp.concatenate([ref[:, :K], ref[:, K:]], axis=0)
        whole[pl.ds(pl.multiple_of(at * (K // 2), K // 2), K // 2), :] = rows
    factor = inverse_factor(whole[...])
    for k in range(OWN):
        out[:, k * TILE : (k + 1) * TILE] = times(factor, image[tile_rows(k), :])


def spread(value, axis):
    return [value] + [swap(value, axis, s) for s in (1, 2, 3)]


def swapped(values, axis):
    arrived = {s: swap(value, axis, s) for s, value in zip(SEND, values)}
    return [arrived[s] for s in (3, 2, 1)]


def body(start_vectors, bucket_weight, tile_count, tile_coords, patterns):
    place = jnp.stack([lax.axis_index(a) for a in DOC_BKT] + [tile_count[0, 0]]).astype(jnp.int32)
    coords = tile_coords.reshape(2 * SLOTS)
    weight = bucket_weight.reshape(COL_TILES, TILE)
    chunk_b = shape(CHUNK, TILE, dtype=bf16)

    pattern, doc_part, sizes = prep(place, coords, weight, patterns.reshape(SLOTS, TILE, TILE))
    payload = call(pack_kernel, "pack", shape(CHUNK + PACKED, TILE, dtype=bf16), [VMEM] * 2)(start_vectors, doc_part)
    turned = call(turn_kernel, "turn", shape(SLOTS, TILE, TILE, dtype=bf16), [VMEM], limit=4, moved=16 * MIB)(pattern)
    inv = scale = None
    for sweep in range(ITERS):
        first, last = sweep == 0, sweep == ITERS - 1
        blocks = spread(payload, BKT)
        if first:
            keep, send, inv = forward(True, place, coords, blocks, pattern, sizes, turned)
            own, *parts = halves(True, keep, swap(send, CORE, 1))
            (part,) = total(True, own, *swapped(parts, X))
            weighted, scale = call(
                functools.partial(weigh_kernel, True), "weigh", (chunk_b, shape(OWN, TILE)), [SMEM] + [VMEM] * 5
            )(place, *spread(part, Z), weight)
        else:
            keep, send, gram = forward(False, place, coords, blocks, pattern)
            own, *parts, gram = halves(False, keep, gram, swap(send, CORE, 1))
            part, gram = total(False, own, *swapped(parts, X), gram)
            weighted = call(functools.partial(weigh_kernel, False), "weigh", chunk_b, [VMEM] * 6)(
                *spread(part, Z), gram, scale
            )
        mine = spread(weighted, X)
        other = swap(jnp.stack(mine), CORE, 1)
        own, *parts = backward(place, coords, mine, other, turned)
        if not last:
            outs = shape(CHUNK + PACKED, TILE, dtype=bf16)
            scratch = ()
        else:
            outs = (shape(CHUNK, TILE), shape(K // 4, TILE), shape(K // 4, TILE))
            scratch = (pltpu.VMEM((K, K), f32),)
        outs = call(functools.partial(image_kernel, last), "image", outs, [SMEM] + [VMEM] * 5, scratch=scratch)(
            place, own, *swapped(parts, BKT), inv
        )
        if not last:
            payload = outs
    image, keep, send = outs
    half = keep + swap(send, CORE, 1)
    others = (X, Z, BKT)
    copies = jnp.broadcast_to(half, (lax.axis_size(others), *half.shape))
    parts = lax.all_to_all(copies, others, split_axis=0, concat_axis=0, tiled=True)
    half = call(sum_kernel, "sum", shape(K // 4, TILE), [VMEM])(parts)
    return call(
        solve_kernel,
        "solve",
        shape(K, OWN * TILE),
        [SMEM] + [VMEM] * 3,
        scratch=[pltpu.VMEM((K, K), f32)],
    )(place, half, swap(half, CORE, 1), image)


def solution(mesh):
    split = Mesh(mesh.devices.reshape(4, 4, 2, mesh.shape[BKT]), DOC_BKT)
    in_specs = (
        P(None, DOC_BKT),
        P(BKT),
        P(DOC, BKT),
        P(DOC, BKT, None, None),
        P(DOC, BKT, None, None, None),
    )
    return jax.shard_map(body, mesh=split, in_specs=in_specs, out_specs=P(None, DOC_BKT), check_vma=False)
```

```python
import functools

import jax
import jax.numpy as jnp
from jax import lax
from jax.experimental import pallas as pl
from jax.experimental.pallas import tpu as pltpu
from jax.sharding import Mesh
from jax.sharding import PartitionSpec as P

ITERS = 2
K = 64
TILE = 128
SLOTS = 256
ROW_TILES = 32
COL_TILES = 64
TOTAL_DOCS = 131072
OWN = 8
CHUNK = OWN * K
COUNT_ROWS = 16
PACKED = 96
TURN = 32
SEND = (1, 2, 3)
PIVOTS = 8
UNROLL = 128
PREP_STEP = 32
MIB = 1 << 20
PREP_LIMIT = 32 * MIB

X, Z, CORE, BKT = "doc_0", "doc_1", "doc_2", "bkt"
DOC = (X, Z, CORE)
DOC_BKT = (X, Z, CORE, BKT)

f32 = jnp.float32
bf16 = jnp.bfloat16
SMEM = pl.BlockSpec(memory_space=pltpu.SMEM)
VMEM = pl.BlockSpec(memory_space=pltpu.VMEM)
HIGHEST = lax.Precision.HIGHEST


def shape(*lengths, dtype=f32):
    return jax.ShapeDtypeStruct(lengths, dtype)


def call(kernel, name, out_shape, in_specs, scratch=(), limit=8, flops=0, moved=0):
    return pl.pallas_call(
        kernel,
        out_shape=out_shape,
        in_specs=in_specs,
        out_specs=jax.tree.map(lambda _: VMEM, out_shape),
        scratch_shapes=list(scratch),
        compiler_params=pltpu.CompilerParams(vmem_limit_bytes=limit * MIB),
        cost_estimate=pl.CostEstimate(flops=flops, bytes_accessed=moved, transcendentals=0),
        name=name,
    )


def swap(value, axis, mask):
    size = lax.axis_size(axis)
    return lax.ppermute(value, axis, [(i, i ^ mask) for i in range(size)])


def place_of(place):
    return place[0], place[1], place[2], place[3], place[4]


def tile_rows(k):
    return slice(k * K, (k + 1) * K)


def split3(value):
    high = value.astype(bf16)
    rest = value - high.astype(f32)
    middle = rest.astype(bf16)
    return high, middle, (rest - middle.astype(f32)).astype(bf16)


def times(factor, value):
    f_high, f_low, _ = split3(factor)
    v_high, v_low, _ = split3(value)
    both = jnp.dot(jnp.concatenate([f_high, f_low], axis=0), v_high, preferred_element_type=f32)
    low = jnp.dot(f_high, v_low, preferred_element_type=f32)
    return both[:K] + (both[K:] + low)


def pack_gram(gram):
    high, middle, low = (term.astype(f32) for term in split3(gram))
    top = jnp.concatenate([high, middle], axis=1)
    bottom = jnp.concatenate([low[: K // 2], low[K // 2 :]], axis=1)
    return jnp.concatenate([top, bottom], axis=0).astype(bf16)


def unpack_gram(packed):
    packed = packed.astype(f32)
    low = jnp.concatenate([packed[K:, :K], packed[K:, K:]], axis=0)
    return (packed[:K, :K] + packed[:K, K:]) + low


def prep_kernel(
    place, coords, weight, pattern_hbm,
    pattern, doc_part, size_part,
    raw, split, doc_acc, size_acc, sems,
):
    steps = SLOTS // PREP_STEP

    def fetch(step):
        at = pl.ds(step * PREP_STEP, PREP_STEP)
        return pltpu.make_async_copy(pattern_hbm.at[at], raw.at[at], sems.at[step])

    for step in range(steps):
        fetch(step).start()
    doc_acc[...] = jnp.zeros_like(doc_acc)
    size_acc[...] = jnp.zeros_like(size_acc)
    rows = lax.broadcasted_iota(jnp.int32, split.shape, 1)
    terms = jnp.zeros(split.shape, f32)
    for i, term in enumerate(split3(weight[...])):
        terms = jnp.where(rows == i, jnp.broadcast_to(term.astype(f32)[:, None, :], split.shape), terms)
    split[...] = terms.astype(bf16)
    count = place[4]

    def block(step, carry):
        fetch(step).wait()
        products, sums = [], []
        for u in range(PREP_STEP):
            slot = step * PREP_STEP + u
            tile = jnp.where(slot < count, raw[slot], 0).astype(f32)
            sums.append(jnp.sum(tile.reshape(TILE // 8, 8, TILE), axis=0))
            tile = tile.astype(bf16)
            pattern[slot] = tile
            products.append(
                lax.dot_general(
                    split[coords[2 * slot + 1]], tile, (((1,), (1,)), ((), ())), preferred_element_type=f32
                )
            )
        for u in range(PREP_STEP):
            slot = step * PREP_STEP + u
            doc_acc[coords[2 * slot]] += products[u]
            size_acc[coords[2 * slot + 1]] += sums[u]
        return carry

    lax.fori_loop(0, steps, block, 0)
    doc_part[...] = jnp.sum(doc_acc[...], axis=1)
    size_part[...] = jnp.sum(size_acc[...], axis=1)


def pack_kernel(vectors, doc_part, payload):
    for k in range(OWN):
        payload[tile_rows(k), :] = vectors[:, k * TILE : (k + 1) * TILE].astype(bf16)
    for i, term in enumerate(split3(doc_part[...])):
        payload[CHUNK + i * ROW_TILES : CHUNK + (i + 1) * ROW_TILES, :] = term


def prep(place, coords, weight, patterns):
    return pl.pallas_call(
        prep_kernel,
        out_shape=(
            shape(SLOTS, TILE, TILE, dtype=bf16),
            shape(ROW_TILES, TILE),
            shape(COL_TILES, TILE),
        ),
        in_specs=[SMEM, SMEM, VMEM, pl.BlockSpec(memory_space=pltpu.HBM)],
        out_specs=(VMEM, VMEM, VMEM),
        scratch_shapes=[
            pltpu.VMEM((SLOTS, TILE, TILE), jnp.int32),
            pltpu.VMEM((COL_TILES, 16, TILE), bf16),
            pltpu.VMEM((ROW_TILES, 16, TILE), f32),
            pltpu.VMEM((COL_TILES, 8, TILE), f32),
            pltpu.SemaphoreType.DMA((SLOTS // PREP_STEP,)),
        ],
        compiler_params=pltpu.CompilerParams(vmem_limit_bytes=PREP_LIMIT),
        cost_estimate=pl.CostEstimate(flops=10**9, bytes_accessed=24 * MIB, transcendentals=0),
        name="prep",
    )(place, coords, weight, patterns)


def turn_kernel(pattern, turned):
    def group(g, carry):
        for u in range(TURN):
            slot = g * TURN + u
            turned[slot] = pattern[slot].T
        return carry

    lax.fori_loop(0, SLOTS // TURN, group, 0)


def tile_products(coords, pattern, source, acc, read, write):
    acc[...] = jnp.zeros_like(acc)

    def group(g, carry):
        products = []
        for u in range(UNROLL):
            slot = g * UNROLL + u
            products.append(
                jnp.dot(source[coords[2 * slot + read]], pattern[slot], preferred_element_type=f32)
            )
        for u in range(UNROLL):
            slot = g * UNROLL + u
            acc[coords[2 * slot + write]] += products[u]
        return carry

    lax.fori_loop(0, SLOTS // UNROLL, group, 0)


def forward_kernel(first, place, coords, b0, b1, b2, b3, pattern, *refs):
    if first:
        sizes, _, keep, send, inv, source, acc = refs
    else:
        keep, send, gram, source, acc = refs
    x, z, c, y, _ = place_of(place)
    blocks = (b0, b1, b2, b3)
    if first:
        terms = [block[CHUNK + i * ROW_TILES : CHUNK + (i + 1) * ROW_TILES, :].astype(f32) for block in blocks for i in range(3)]
        parts = [(terms[3 * s] + terms[3 * s + 1]) + terms[3 * s + 2] for s in range(4)]
        inv[...] = 1.0 / jnp.sqrt(jnp.maximum((parts[0] + parts[1]) + (parts[2] + parts[3]), 1.0))
    for s, block in enumerate(blocks):
        base = (y ^ s) * OWN
        for k in range(OWN):
            tile = block[tile_rows(k), :]
            if first:
                tile = (tile.astype(f32) * inv[pl.ds(base + k, 1), :]).astype(bf16)
            source[base + k] = tile
    tile_products(coords, pattern, source, acc, 0, 1)
    for out, half in ((keep, c), (send, 1 - c)):
        for r in range(4):
            base = half * (COL_TILES // 2) + (x ^ r) * OWN
            for k in range(OWN):
                at = r * CHUNK + k * K
                out[at : at + K, :] = acc[base + k].astype(out.dtype)
            if first:
                counts = jnp.concatenate(
                    [sizes[pl.ds(pl.multiple_of(base, OWN), OWN), :], jnp.zeros((COUNT_ROWS - OWN, TILE), f32)], axis=0
                )
                at = 4 * CHUNK + r * COUNT_ROWS
                out[at : at + COUNT_ROWS, :] = counts.astype(out.dtype)
    if not first:
        parts = [unpack_gram(block[CHUNK : CHUNK + PACKED, :]) for block in blocks]
        gram[...] = (parts[0] + parts[1]) + (parts[2] + parts[3])
        send[4 * CHUNK : 4 * CHUNK + PACKED, :] = pack_gram(gram[...])


def forward(first, place, coords, blocks, pattern, *sizes):
    extra = 4 * COUNT_ROWS
    outs = (
        shape(4 * CHUNK + (extra if first else 0), TILE),
        shape(4 * CHUNK + (extra if first else PACKED), TILE, dtype=bf16),
        shape(ROW_TILES, TILE) if first else shape(K, K),
    )
    return call(
        functools.partial(forward_kernel, first),
        "forward",
        outs,
        [SMEM, SMEM] + [VMEM] * (5 + len(sizes)),
        scratch=[pltpu.VMEM((ROW_TILES, K, TILE), bf16), pltpu.VMEM((COL_TILES, K, TILE), f32)],
        limit=20,
        flops=6 * 10**9,
        moved=12 * MIB,
    )(place, coords, *blocks, pattern, *sizes)


def halves_kernel(first, *refs):
    if first:
        keep, arrived, own, *sent = refs
    else:
        keep, gram, arrived, own, *sent, gram_out = refs
        gram_out[...] = gram[...] + unpack_gram(arrived[4 * CHUNK : 4 * CHUNK + PACKED, :])
        packed = pack_gram(gram_out[...])
    for r, out in ((0, own), *zip(SEND, sent)):
        at = slice(r * CHUNK, (r + 1) * CHUNK)
        out[:CHUNK, :] = (keep[at, :] + arrived[at, :].astype(f32)).astype(out.dtype)
        if first:
            at = slice(4 * CHUNK + r * COUNT_ROWS, 4 * CHUNK + (r + 1) * COUNT_ROWS)
            out[CHUNK:, :] = (keep[at, :] + arrived[at, :].astype(f32)).astype(out.dtype)
        elif r:
            out[CHUNK:, :] = packed


def halves(first, *args):
    rows = CHUNK + (COUNT_ROWS if first else PACKED)
    outs = [shape(rows if first else CHUNK, TILE)] + [shape(rows, TILE, dtype=bf16)] * 3
    if not first:
        outs.append(shape(K, K))
    return call(functools.partial(halves_kernel, first), "halves", tuple(outs), [VMEM] * len(args), moved=3 * MIB)(*args)


def add4(own, r1, r2, r3, at):
    return (own[at, :].astype(f32) + r1[at, :].astype(f32)) + (r2[at, :].astype(f32) + r3[at, :].astype(f32))


def add_grams(gram, *refs):
    parts = [unpack_gram(ref[CHUNK : CHUNK + PACKED, :]) for ref in refs]
    return (gram[...] + parts[0]) + (parts[1] + parts[2])


def total_kernel(first, *refs):
    if first:
        own, r1, r2, r3, out = refs
        out[...] = add4(own, r1, r2, r3, slice(None)).astype(bf16)
    else:
        own, r1, r2, r3, gram, out, gram_out = refs
        out[:CHUNK, :] = add4(own, r1, r2, r3, slice(0, CHUNK)).astype(bf16)
        gram_out[...] = add_grams(gram, r1, r2, r3)
        out[CHUNK:, :] = pack_gram(gram_out[...])


def total(first, *args):
    rows = CHUNK + (COUNT_ROWS if first else PACKED)
    outs = (shape(rows, TILE, dtype=bf16),) + (() if first else (shape(K, K),))
    return call(functools.partial(total_kernel, first), "total", outs, [VMEM] * len(args))(*args)


def inverse_factor(gram):
    work = jnp.concatenate([gram, jnp.eye(K, dtype=f32)], axis=1)
    below = lax.broadcasted_iota(jnp.int32, (K, 1), 0)
    for k in range(0, K, PIVOTS):
        cols = [jnp.broadcast_to(work[:, k + j : k + j + 1], (K, 2 * K)) for j in range(PIVOTS)]
        rows = [work[k + j : k + j + 1, :] for j in range(PIVOTS)]
        for j in range(PIVOTS):
            inverse = 1.0 / cols[j][k + j : k + j + 1, :]
            row = rows[j] * inverse
            for i in range(j + 1, PIVOTS):
                factor = cols[j][k + i : k + i + 1, :]
                rows[i] = rows[i] - factor * row
                cols[i] = cols[i] - cols[j] * (factor * inverse)
            work = work - jnp.where(below > k + j, cols[j], 0.0) * row
    diagonal = lax.broadcasted_iota(jnp.int32, (K, K), 0) == lax.broadcasted_iota(jnp.int32, (K, K), 1)
    pivots = jnp.sum(jnp.where(diagonal, work[:, :K], 0.0), axis=1, keepdims=True)
    return work[:, K:] / jnp.sqrt(pivots)


def weigh_kernel(first, *refs):
    if first:
        place, p0, p1, p2, p3, weight, weighted, scale = refs
        x, z, c, y, _ = place_of(place)
        base = pl.multiple_of(c * (COL_TILES // 2) + x * OWN, OWN)
        counts = add4(p0, p1, p2, p3, slice(CHUNK, CHUNK + COUNT_ROWS))[:OWN]
        scale[...] = weight[pl.ds(base, OWN), :] / jnp.maximum(counts, 1.0)
    else:
        p0, p1, p2, p3, gram, scale, weighted = refs
        factor = inverse_factor(add_grams(gram, p1, p2, p3))
    for k in range(OWN):
        tile = add4(p0, p1, p2, p3, tile_rows(k))
        if not first:
            tile = times(factor, tile)
        weighted[tile_rows(k), :] = (tile * scale[k : k + 1, :]).astype(bf16)


def backward_kernel(place, coords, w0, w1, w2, w3, other, turned, own, s1, s2, s3, source, acc):
    sent = (s1, s2, s3)
    x, z, c, y, _ = place_of(place)
    for r, block in enumerate((w0, w1, w2, w3)):
        base = c * (COL_TILES // 2) + (x ^ r) * OWN
        far = (1 - c) * (COL_TILES // 2) + (x ^ r) * OWN
        for k in range(OWN):
            source[base + k] = block[tile_rows(k), :]
            source[far + k] = other[r, tile_rows(k), :]
    tile_products(coords, turned, source, acc, 1, 0)
    for s, out in ((0, own), *zip(SEND, sent)):
        base = (y ^ s) * OWN
        for k in range(OWN):
            out[tile_rows(k), :] = acc[base + k].astype(out.dtype)


def backward(place, coords, blocks, other, turned):
    outs = [shape(CHUNK, TILE)] + [shape(CHUNK, TILE, dtype=bf16)] * 3
    return call(
        backward_kernel,
        "backward",
        tuple(outs),
        [SMEM, SMEM] + [VMEM] * 6,
        scratch=[pltpu.VMEM((COL_TILES, K, TILE), bf16), pltpu.VMEM((ROW_TILES, K, TILE), f32)],
        limit=20,
        flops=6 * 10**9,
        moved=12 * MIB,
    )(place, coords, *blocks, other, turned)


def image_kernel(last, place, own, r1, r2, r3, inv, *refs):
    x, z, c, y, _ = place_of(place)
    inv_own = inv[pl.ds(pl.multiple_of(y * OWN, OWN), OWN), :]
    gram = jnp.zeros((K, K), f32)
    for k in range(OWN):
        at = tile_rows(k)
        tile = add4(own, r1, r2, r3, at) * inv_own[k : k + 1, :]
        if last:
            refs[0][at, :] = tile
        else:
            refs[0][at, :] = (tile * inv_own[k : k + 1, :]).astype(bf16)
        gram += lax.dot_general(
            tile, tile, (((1,), (1,)), ((), ())), precision=HIGHEST, preferred_element_type=f32
        )
    gram = gram / TOTAL_DOCS
    if last:
        image, halves_beside = refs
        halves_beside[...] = jnp.concatenate([gram[: K // 2], gram[K // 2 :]], axis=1)
    else:
        refs[0][CHUNK:, :] = pack_gram(gram)


def sum_kernel(own, r1, r3, r2, out):
    out[...] = (own[...] + r1[...]) + (r2[...] + r3[...])


def solve_kernel(gram, image, out):
    factor = inverse_factor(jnp.concatenate([gram[:, :K], gram[:, K:]], axis=0))
    for k in range(OWN):
        out[:, k * TILE : (k + 1) * TILE] = times(factor, image[tile_rows(k), :])


def spread(value, axis):
    return [value] + [swap(value, axis, s) for s in (1, 2, 3)]


def swapped(values, axis):
    arrived = {s: swap(value, axis, s) for s, value in zip(SEND, values)}
    return [arrived[s] for s in (3, 2, 1)]


def body(start_vectors, bucket_weight, tile_count, tile_coords, patterns):
    place = jnp.stack([lax.axis_index(a) for a in DOC_BKT] + [tile_count[0, 0]]).astype(jnp.int32)
    coords = tile_coords.reshape(2 * SLOTS)
    weight = bucket_weight.reshape(COL_TILES, TILE)
    chunk_b = shape(CHUNK, TILE, dtype=bf16)

    pattern, doc_part, sizes = prep(place, coords, weight, patterns.reshape(SLOTS, TILE, TILE))
    payload = call(pack_kernel, "pack", shape(CHUNK + PACKED, TILE, dtype=bf16), [VMEM] * 2)(start_vectors, doc_part)
    turned = call(turn_kernel, "turn", shape(SLOTS, TILE, TILE, dtype=bf16), [VMEM], limit=4, moved=16 * MIB)(pattern)
    inv = scale = None
    for sweep in range(ITERS):
        first, last = sweep == 0, sweep == ITERS - 1
        blocks = spread(payload, BKT)
        if first:
            keep, send, inv = forward(True, place, coords, blocks, pattern, sizes, turned)
            own, *parts = halves(True, keep, swap(send, CORE, 1))
            (part,) = total(True, own, *swapped(parts, X))
            weighted, scale = call(
                functools.partial(weigh_kernel, True), "weigh", (chunk_b, shape(OWN, TILE)), [SMEM] + [VMEM] * 5
            )(place, *spread(part, Z), weight)
        else:
            keep, send, gram = forward(False, place, coords, blocks, pattern)
            own, *parts, gram = halves(False, keep, gram, swap(send, CORE, 1))
            part, gram = total(False, own, *swapped(parts, X), gram)
            weighted = call(functools.partial(weigh_kernel, False), "weigh", chunk_b, [VMEM] * 6)(
                *spread(part, Z), gram, scale
            )
        mine = spread(weighted, X)
        other = swap(jnp.stack(mine), CORE, 1)
        own, *parts = backward(place, coords, mine, other, turned)
        if not last:
            outs = shape(CHUNK + PACKED, TILE, dtype=bf16)
        else:
            outs = (shape(CHUNK, TILE), shape(K // 2, 2 * K))
        outs = call(functools.partial(image_kernel, last), "image", outs, [SMEM] + [VMEM] * 5)(
            place, own, *swapped(parts, BKT), inv
        )
        if not last:
            payload = outs
    image, gram = outs
    gram = gram + swap(gram, CORE, 1)
    for axis in (BKT, X, Z):
        gram = call(sum_kernel, "sum", shape(K // 2, 2 * K), [VMEM] * 4)(
            gram, *[swap(gram, axis, s) for s in (1, 3, 2)]
        )
    return call(solve_kernel, "solve", shape(K, OWN * TILE), [VMEM] * 2)(gram, image)


def solution(mesh):
    split = Mesh(mesh.devices.reshape(4, 4, 2, mesh.shape[BKT]), DOC_BKT)
    in_specs = (
        P(None, DOC_BKT),
        P(BKT),
        P(DOC, BKT),
        P(DOC, BKT, None, None),
        P(DOC, BKT, None, None, None),
    )
    return jax.shard_map(body, mesh=split, in_specs=in_specs, out_specs=P(None, DOC_BKT), check_vma=False)
```

```python
import functools

import jax
import jax.numpy as jnp
from jax import lax
from jax.experimental import pallas as pl
from jax.experimental.pallas import tpu as pltpu
from jax.sharding import Mesh
from jax.sharding import PartitionSpec as P

ITERS = 2
K = 64
TILE = 128
SLOTS = 256
ROW_TILES = 32
COL_TILES = 64
TOTAL_DOCS = 131072
OWN = 8
CHUNK = OWN * K
COUNT_ROWS = 16
PACKED = 96
TURN = 32
SEND = (1, 2, 3)
PIVOTS = 8
UNROLL = 256
PREP_STEP = 32
MIB = 1 << 20
PREP_LIMIT = 32 * MIB

X, Z, CORE, BKT = "doc_0", "doc_1", "doc_2", "bkt"
DOC = (X, Z, CORE)
DOC_BKT = (X, Z, CORE, BKT)

f32 = jnp.float32
bf16 = jnp.bfloat16
SMEM = pl.BlockSpec(memory_space=pltpu.SMEM)
VMEM = pl.BlockSpec(memory_space=pltpu.VMEM)
HIGHEST = lax.Precision.HIGHEST


def shape(*lengths, dtype=f32):
    return jax.ShapeDtypeStruct(lengths, dtype)


def call(kernel, name, out_shape, in_specs, scratch=(), limit=8, flops=0, moved=0):
    return pl.pallas_call(
        kernel,
        out_shape=out_shape,
        in_specs=in_specs,
        out_specs=jax.tree.map(lambda _: VMEM, out_shape),
        scratch_shapes=list(scratch),
        compiler_params=pltpu.CompilerParams(vmem_limit_bytes=limit * MIB),
        cost_estimate=pl.CostEstimate(flops=flops, bytes_accessed=moved, transcendentals=0),
        name=name,
    )


def swap(value, axis, mask):
    size = lax.axis_size(axis)
    return lax.ppermute(value, axis, [(i, i ^ mask) for i in range(size)])


def place_of(place):
    return place[0], place[1], place[2], place[3], place[4]


def tile_rows(k):
    return slice(k * K, (k + 1) * K)


def split3(value):
    high = value.astype(bf16)
    rest = value - high.astype(f32)
    middle = rest.astype(bf16)
    return high, middle, (rest - middle.astype(f32)).astype(bf16)


def times(factor, value):
    f_high, f_low, _ = split3(factor)
    v_high, v_low, _ = split3(value)
    both = jnp.dot(jnp.concatenate([f_high, f_low], axis=0), v_high, preferred_element_type=f32)
    low = jnp.dot(f_high, v_low, preferred_element_type=f32)
    return both[:K] + (both[K:] + low)


def pack_gram(gram):
    high, middle, low = (term.astype(f32) for term in split3(gram))
    top = jnp.concatenate([high, middle], axis=1)
    bottom = jnp.concatenate([low[: K // 2], low[K // 2 :]], axis=1)
    return jnp.concatenate([top, bottom], axis=0).astype(bf16)


def unpack_gram(packed):
    packed = packed.astype(f32)
    low = jnp.concatenate([packed[K:, :K], packed[K:, K:]], axis=0)
    return (packed[:K, :K] + packed[:K, K:]) + low


def prep_kernel(
    place, coords, weight, pattern_hbm,
    pattern, doc_part, size_part,
    raw, split, doc_acc, size_acc, sems,
):
    steps = SLOTS // PREP_STEP

    def fetch(step):
        at = pl.ds(step * PREP_STEP, PREP_STEP)
        return pltpu.make_async_copy(pattern_hbm.at[at], raw.at[at], sems.at[step])

    for step in range(steps):
        fetch(step).start()
    doc_acc[...] = jnp.zeros_like(doc_acc)
    size_acc[...] = jnp.zeros_like(size_acc)
    rows = lax.broadcasted_iota(jnp.int32, split.shape, 1)
    terms = jnp.zeros(split.shape, f32)
    for i, term in enumerate(split3(weight[...])):
        terms = jnp.where(rows == i, jnp.broadcast_to(term.astype(f32)[:, None, :], split.shape), terms)
    split[...] = terms.astype(bf16)
    count = place[4]

    def block(step, carry):
        fetch(step).wait()
        products, sums = [], []
        for u in range(PREP_STEP):
            slot = step * PREP_STEP + u
            tile = jnp.where(slot < count, raw[slot], 0).astype(f32)
            sums.append(jnp.sum(tile.reshape(TILE // 8, 8, TILE), axis=0))
            tile = tile.astype(bf16)
            pattern[slot] = tile
            products.append(
                lax.dot_general(
                    split[coords[2 * slot + 1]], tile, (((1,), (1,)), ((), ())), preferred_element_type=f32
                )
            )
        for u in range(PREP_STEP):
            slot = step * PREP_STEP + u
            doc_acc[coords[2 * slot]] += products[u]
            size_acc[coords[2 * slot + 1]] += sums[u]
        return carry

    lax.fori_loop(0, steps, block, 0)
    doc_part[...] = jnp.sum(doc_acc[...], axis=1)
    size_part[...] = jnp.sum(size_acc[...], axis=1)


def pack_kernel(vectors, doc_part, payload):
    for k in range(OWN):
        payload[tile_rows(k), :] = vectors[:, k * TILE : (k + 1) * TILE].astype(bf16)
    for i, term in enumerate(split3(doc_part[...])):
        payload[CHUNK + i * ROW_TILES : CHUNK + (i + 1) * ROW_TILES, :] = term


def prep(place, coords, weight, patterns):
    return pl.pallas_call(
        prep_kernel,
        out_shape=(
            shape(SLOTS, TILE, TILE, dtype=bf16),
            shape(ROW_TILES, TILE),
            shape(COL_TILES, TILE),
        ),
        in_specs=[SMEM, SMEM, VMEM, pl.BlockSpec(memory_space=pltpu.HBM)],
        out_specs=(VMEM, VMEM, VMEM),
        scratch_shapes=[
            pltpu.VMEM((SLOTS, TILE, TILE), jnp.int32),
            pltpu.VMEM((COL_TILES, 16, TILE), bf16),
            pltpu.VMEM((ROW_TILES, 16, TILE), f32),
            pltpu.VMEM((COL_TILES, 8, TILE), f32),
            pltpu.SemaphoreType.DMA((SLOTS // PREP_STEP,)),
        ],
        compiler_params=pltpu.CompilerParams(vmem_limit_bytes=PREP_LIMIT),
        cost_estimate=pl.CostEstimate(flops=10**9, bytes_accessed=24 * MIB, transcendentals=0),
        name="prep",
    )(place, coords, weight, patterns)


def turn_kernel(pattern, turned):
    def group(g, carry):
        for u in range(TURN):
            slot = g * TURN + u
            turned[slot] = pattern[slot].T
        return carry

    lax.fori_loop(0, SLOTS // TURN, group, 0)


def tile_products(coords, pattern, source, acc, read, write):
    acc[...] = jnp.zeros_like(acc)

    def group(g, carry):
        products = []
        for u in range(UNROLL):
            slot = g * UNROLL + u
            products.append(
                jnp.dot(source[coords[2 * slot + read]], pattern[slot], preferred_element_type=f32)
            )
        for u in range(UNROLL):
            slot = g * UNROLL + u
            acc[coords[2 * slot + write]] += products[u]
        return carry

    lax.fori_loop(0, SLOTS // UNROLL, group, 0)


def forward_kernel(first, place, coords, b0, b1, b2, b3, pattern, *refs):
    if first:
        sizes, _, keep, send, inv, source, acc = refs
    else:
        keep, send, gram, source, acc = refs
    x, z, c, y, _ = place_of(place)
    blocks = (b0, b1, b2, b3)
    if first:
        terms = [block[CHUNK + i * ROW_TILES : CHUNK + (i + 1) * ROW_TILES, :].astype(f32) for block in blocks for i in range(3)]
        parts = [(terms[3 * s] + terms[3 * s + 1]) + terms[3 * s + 2] for s in range(4)]
        inv[...] = 1.0 / jnp.sqrt(jnp.maximum((parts[0] + parts[1]) + (parts[2] + parts[3]), 1.0))
    for s, block in enumerate(blocks):
        base = (y ^ s) * OWN
        for k in range(OWN):
            tile = block[tile_rows(k), :]
            if first:
                tile = (tile.astype(f32) * inv[pl.ds(base + k, 1), :]).astype(bf16)
            source[base + k] = tile
    tile_products(coords, pattern, source, acc, 0, 1)
    for out, half in ((keep, c), (send, 1 - c)):
        for r in range(4):
            base = half * (COL_TILES // 2) + (x ^ r) * OWN
            for k in range(OWN):
                at = r * CHUNK + k * K
                out[at : at + K, :] = acc[base + k].astype(out.dtype)
            if first:
                counts = jnp.concatenate(
                    [sizes[pl.ds(pl.multiple_of(base, OWN), OWN), :], jnp.zeros((COUNT_ROWS - OWN, TILE), f32)], axis=0
                )
                at = 4 * CHUNK + r * COUNT_ROWS
                out[at : at + COUNT_ROWS, :] = counts.astype(out.dtype)
    if not first:
        parts = [unpack_gram(block[CHUNK : CHUNK + PACKED, :]) for block in blocks]
        gram[...] = (parts[0] + parts[1]) + (parts[2] + parts[3])
        send[4 * CHUNK : 4 * CHUNK + PACKED, :] = pack_gram(gram[...])


def forward(first, place, coords, blocks, pattern, *sizes):
    extra = 4 * COUNT_ROWS
    outs = (
        shape(4 * CHUNK + (extra if first else 0), TILE),
        shape(4 * CHUNK + (extra if first else PACKED), TILE, dtype=bf16),
        shape(ROW_TILES, TILE) if first else shape(K, K),
    )
    return call(
        functools.partial(forward_kernel, first),
        "forward",
        outs,
        [SMEM, SMEM] + [VMEM] * (5 + len(sizes)),
        scratch=[pltpu.VMEM((ROW_TILES, K, TILE), bf16), pltpu.VMEM((COL_TILES, K, TILE), f32)],
        limit=20,
        flops=6 * 10**9,
        moved=12 * MIB,
    )(place, coords, *blocks, pattern, *sizes)


def halves_kernel(first, *refs):
    if first:
        keep, arrived, own, *sent = refs
    else:
        keep, gram, arrived, own, *sent, gram_out = refs
        gram_out[...] = gram[...] + unpack_gram(arrived[4 * CHUNK : 4 * CHUNK + PACKED, :])
        packed = pack_gram(gram_out[...])
    for r, out in ((0, own), *zip(SEND, sent)):
        at = slice(r * CHUNK, (r + 1) * CHUNK)
        out[:CHUNK, :] = (keep[at, :] + arrived[at, :].astype(f32)).astype(out.dtype)
        if first:
            at = slice(4 * CHUNK + r * COUNT_ROWS, 4 * CHUNK + (r + 1) * COUNT_ROWS)
            out[CHUNK:, :] = (keep[at, :] + arrived[at, :].astype(f32)).astype(out.dtype)
        elif r:
            out[CHUNK:, :] = packed


def halves(first, *args):
    rows = CHUNK + (COUNT_ROWS if first else PACKED)
    outs = [shape(rows if first else CHUNK, TILE)] + [shape(rows, TILE, dtype=bf16)] * 3
    if not first:
        outs.append(shape(K, K))
    return call(functools.partial(halves_kernel, first), "halves", tuple(outs), [VMEM] * len(args), moved=3 * MIB)(*args)


def add4(own, r1, r2, r3, at):
    return (own[at, :].astype(f32) + r1[at, :].astype(f32)) + (r2[at, :].astype(f32) + r3[at, :].astype(f32))


def add_grams(gram, *refs):
    parts = [unpack_gram(ref[CHUNK : CHUNK + PACKED, :]) for ref in refs]
    return (gram[...] + parts[0]) + (parts[1] + parts[2])


def total_kernel(first, *refs):
    if first:
        own, r1, r2, r3, out = refs
        out[...] = add4(own, r1, r2, r3, slice(None)).astype(bf16)
    else:
        own, r1, r2, r3, gram, out, gram_out = refs
        out[:CHUNK, :] = add4(own, r1, r2, r3, slice(0, CHUNK)).astype(bf16)
        gram_out[...] = add_grams(gram, r1, r2, r3)
        out[CHUNK:, :] = pack_gram(gram_out[...])


def total(first, *args):
    rows = CHUNK + (COUNT_ROWS if first else PACKED)
    outs = (shape(rows, TILE, dtype=bf16),) + (() if first else (shape(K, K),))
    return call(functools.partial(total_kernel, first), "total", outs, [VMEM] * len(args))(*args)


def inverse_factor(gram):
    work = jnp.concatenate([gram, jnp.eye(K, dtype=f32)], axis=1)
    below = lax.broadcasted_iota(jnp.int32, (K, 1), 0)
    for k in range(0, K, PIVOTS):
        cols = [jnp.broadcast_to(work[:, k + j : k + j + 1], (K, 2 * K)) for j in range(PIVOTS)]
        rows = [work[k + j : k + j + 1, :] for j in range(PIVOTS)]
        for j in range(PIVOTS):
            inverse = 1.0 / cols[j][k + j : k + j + 1, :]
            row = rows[j] * inverse
            for i in range(j + 1, PIVOTS):
                factor = cols[j][k + i : k + i + 1, :]
                rows[i] = rows[i] - factor * row
                cols[i] = cols[i] - cols[j] * (factor * inverse)
            work = work - jnp.where(below > k + j, cols[j], 0.0) * row
    diagonal = lax.broadcasted_iota(jnp.int32, (K, K), 0) == lax.broadcasted_iota(jnp.int32, (K, K), 1)
    pivots = jnp.sum(jnp.where(diagonal, work[:, :K], 0.0), axis=1, keepdims=True)
    return work[:, K:] / jnp.sqrt(pivots)


def weigh_kernel(first, *refs):
    if first:
        place, p0, p1, p2, p3, weight, weighted, scale = refs
        x, z, c, y, _ = place_of(place)
        base = pl.multiple_of(c * (COL_TILES // 2) + x * OWN, OWN)
        counts = add4(p0, p1, p2, p3, slice(CHUNK, CHUNK + COUNT_ROWS))[:OWN]
        scale[...] = weight[pl.ds(base, OWN), :] / jnp.maximum(counts, 1.0)
    else:
        p0, p1, p2, p3, gram, scale, weighted = refs
        factor = inverse_factor(add_grams(gram, p1, p2, p3))
    for k in range(OWN):
        tile = add4(p0, p1, p2, p3, tile_rows(k))
        if not first:
            tile = times(factor, tile)
        weighted[tile_rows(k), :] = (tile * scale[k : k + 1, :]).astype(bf16)


def backward_kernel(place, coords, w0, w1, w2, w3, other, turned, own, s1, s2, s3, source, acc):
    sent = (s1, s2, s3)
    x, z, c, y, _ = place_of(place)
    for r, block in enumerate((w0, w1, w2, w3)):
        base = c * (COL_TILES // 2) + (x ^ r) * OWN
        far = (1 - c) * (COL_TILES // 2) + (x ^ r) * OWN
        for k in range(OWN):
            source[base + k] = block[tile_rows(k), :]
            source[far + k] = other[r, tile_rows(k), :]
    tile_products(coords, turned, source, acc, 1, 0)
    for s, out in ((0, own), *zip(SEND, sent)):
        base = (y ^ s) * OWN
        for k in range(OWN):
            out[tile_rows(k), :] = acc[base + k].astype(out.dtype)


def backward(place, coords, blocks, other, turned):
    outs = [shape(CHUNK, TILE)] + [shape(CHUNK, TILE, dtype=bf16)] * 3
    return call(
        backward_kernel,
        "backward",
        tuple(outs),
        [SMEM, SMEM] + [VMEM] * 6,
        scratch=[pltpu.VMEM((COL_TILES, K, TILE), bf16), pltpu.VMEM((ROW_TILES, K, TILE), f32)],
        limit=20,
        flops=6 * 10**9,
        moved=12 * MIB,
    )(place, coords, *blocks, other, turned)


def image_kernel(last, place, own, r1, r2, r3, inv, *refs):
    x, z, c, y, _ = place_of(place)
    inv_own = inv[pl.ds(pl.multiple_of(y * OWN, OWN), OWN), :]
    gram = jnp.zeros((K, K), f32)
    for k in range(OWN):
        at = tile_rows(k)
        tile = add4(own, r1, r2, r3, at) * inv_own[k : k + 1, :]
        if last:
            refs[0][at, :] = tile
        else:
            refs[0][at, :] = (tile * inv_own[k : k + 1, :]).astype(bf16)
        gram += lax.dot_general(
            tile, tile, (((1,), (1,)), ((), ())), precision=HIGHEST, preferred_element_type=f32
        )
    gram = gram / TOTAL_DOCS
    if last:
        image, halves_beside = refs
        halves_beside[...] = jnp.concatenate([gram[: K // 2], gram[K // 2 :]], axis=1)
    else:
        refs[0][CHUNK:, :] = pack_gram(gram)


def sum_kernel(own, r1, r3, r2, out):
    out[...] = (own[...] + r1[...]) + (r2[...] + r3[...])


def solve_kernel(gram, image, out):
    factor = inverse_factor(jnp.concatenate([gram[:, :K], gram[:, K:]], axis=0))
    for k in range(OWN):
        out[:, k * TILE : (k + 1) * TILE] = times(factor, image[tile_rows(k), :])


def spread(value, axis):
    return [value] + [swap(value, axis, s) for s in (1, 2, 3)]


def swapped(values, axis):
    arrived = {s: swap(value, axis, s) for s, value in zip(SEND, values)}
    return [arrived[s] for s in (3, 2, 1)]


def body(start_vectors, bucket_weight, tile_count, tile_coords, patterns):
    place = jnp.stack([lax.axis_index(a) for a in DOC_BKT] + [tile_count[0, 0]]).astype(jnp.int32)
    coords = tile_coords.reshape(2 * SLOTS)
    weight = bucket_weight.reshape(COL_TILES, TILE)
    chunk_b = shape(CHUNK, TILE, dtype=bf16)

    pattern, doc_part, sizes = prep(place, coords, weight, patterns.reshape(SLOTS, TILE, TILE))
    payload = call(pack_kernel, "pack", shape(CHUNK + PACKED, TILE, dtype=bf16), [VMEM] * 2)(start_vectors, doc_part)
    turned = call(turn_kernel, "turn", shape(SLOTS, TILE, TILE, dtype=bf16), [VMEM], limit=4, moved=16 * MIB)(pattern)
    inv = scale = None
    for sweep in range(ITERS):
        first, last = sweep == 0, sweep == ITERS - 1
        blocks = spread(payload, BKT)
        if first:
            keep, send, inv = forward(True, place, coords, blocks, pattern, sizes, turned)
            own, *parts = halves(True, keep, swap(send, CORE, 1))
            (part,) = total(True, own, *swapped(parts, X))
            weighted, scale = call(
                functools.partial(weigh_kernel, True), "weigh", (chunk_b, shape(OWN, TILE)), [SMEM] + [VMEM] * 5
            )(place, *spread(part, Z), weight)
        else:
            keep, send, gram = forward(False, place, coords, blocks, pattern)
            own, *parts, gram = halves(False, keep, gram, swap(send, CORE, 1))
            part, gram = total(False, own, *swapped(parts, X), gram)
            weighted = call(functools.partial(weigh_kernel, False), "weigh", chunk_b, [VMEM] * 6)(
                *spread(part, Z), gram, scale
            )
        mine = spread(weighted, X)
        other = swap(jnp.stack(mine), CORE, 1)
        own, *parts = backward(place, coords, mine, other, turned)
        if not last:
            outs = shape(CHUNK + PACKED, TILE, dtype=bf16)
        else:
            outs = (shape(CHUNK, TILE), shape(K // 2, 2 * K))
        outs = call(functools.partial(image_kernel, last), "image", outs, [SMEM] + [VMEM] * 5)(
            place, own, *swapped(parts, BKT), inv
        )
        if not last:
            payload = outs
    image, gram = outs
    gram = gram + swap(gram, CORE, 1)
    for axis in (BKT, X, Z):
        gram = call(sum_kernel, "sum", shape(K // 2, 2 * K), [VMEM] * 4)(
            gram, *[swap(gram, axis, s) for s in (1, 3, 2)]
        )
    return call(solve_kernel, "solve", shape(K, OWN * TILE), [VMEM] * 2)(gram, image)


def solution(mesh):
    split = Mesh(mesh.devices.reshape(4, 4, 2, mesh.shape[BKT]), DOC_BKT)
    in_specs = (
        P(None, DOC_BKT),
        P(BKT),
        P(DOC, BKT),
        P(DOC, BKT, None, None),
        P(DOC, BKT, None, None, None),
    )
    return jax.shard_map(body, mesh=split, in_specs=in_specs, out_specs=P(None, DOC_BKT), check_vma=False)
```
